512 devices in a mesh: rows: 256 (over x, z, y), feat: 2 (over core).
Axes of the slice: x: 4, y: 8, z: 8, core: 2. Of those that a mesh axis runs over, the one named last changes fastest.
Arguments:
- embeddings: bfloat16 [196608, 768], P('rows', 'feat'), may hold values from -6 to 6
- factor: float32 [196608, 256], P(('rows', 'feat')), may hold values from -0.1 to 0.1, as said below
- residual_diag: float32 [196608], P(('rows', 'feat')), may hold values from 0.5 to 1.5
- pivots: int32 [2, 256], replicated, may hold values from 0 to 196607, as said below
Outputs:
- new_columns: float32 [2, 196608, 256], P(None, ('rows', 'feat'))
- residual_out: float32 [196608], P(('rows', 'feat'))
The draws below stay inside these ranges and needn't reach their ends.
Inputs may be any that keep to these rules, and one draw needn't show every extreme that they name: Each block's 256 pivots are distinct and increasing, the two blocks share none, and in each block at most 2 pivots lie among the 768 candidates of one index of rows; some index holds exactly 2 in every block. `factor`: entries are independent.
All inputs are finite; a program needn't handle non-finite values.
Results may differ from the reference program's by a relative error of at most 0.0003.
Values may be sent and summed in bfloat16 or wider, within the bound.
A program may use at most 64 MiB of HBM per device.

```python
import jax
import jax.numpy as jnp
from jax import lax

D = 768
R = 256
B = 256
ROWS_DEV = 768
NCAND = 196608
CAP = 2
N_ROWS = 256


def draw_factor(key, part):
    factor_key = jax.random.fold_in(key, 29)
    values = 0.03 * jax.random.truncated_normal(factor_key, -3.3, 3.3, (NCAND, R), jnp.float32)
    return values.astype(jnp.float32)


def draw_pivots(key, part):
    slot_count = N_ROWS * CAP
    stripe = ROWS_DEV // (2 * CAP)
    block_list = []
    for block_id in range(2):
        block_key = jax.random.fold_in(key, 11 + block_id)
        score_key, full_key, jitter_key = jax.random.split(block_key, 3)
        scores = jax.random.randint(score_key, (slot_count,), 0, 1 << 18)
        slot_ids = jnp.arange(slot_count, dtype=jnp.int32)
        full_device = jax.random.randint(full_key, (), 0, N_ROWS)
        boosted = scores + jnp.where(slot_ids // CAP == full_device, 1 << 19, 0)
        keyed = boosted * slot_count + slot_ids
        top_values, top_slots = lax.top_k(keyed, B)
        device = top_slots // CAP
        slot_pos = top_slots % CAP
        jitter = jax.random.randint(jitter_key, (B,), 0, stripe)
        chosen = device * ROWS_DEV + (block_id * CAP + slot_pos) * stripe + jitter
        block_list.append(jnp.sort(chosen))
    return jnp.stack(block_list).astype(jnp.int32)


def block_levels(rng, extent, shards, least, top_value):
    def one(axis_at, parts):
        steps = jax.random.uniform(jax.random.fold_in(jax.random.fold_in(rng, 6), axis_at), (parts,), jnp.float32, least / len(shards), top_value / len(shards))
        return jnp.repeat(jnp.exp(steps), extent[axis_at] // parts).reshape((-1,) + (1,) * (len(extent) - axis_at - 1))

    gain = one(*shards[0])
    for cut in shards[1:]:
        gain = gain * one(*cut)
    return gain


def bell_draw(key, shape, width, reach, shards=(), held_as=jnp.bfloat16):
    result = jax.random.normal(key, shape, jnp.float32) * width
    if len(shards) > 0:
        result = block_levels(key, shape, shards, -0.22, 0.18) * result
    return jnp.clip(result, min=-reach, max=reach).astype(held_as)


def setup_inputs(seed: int = 0) -> dict:
    splits = jax.random.split(jax.random.key(seed), 5)
    return {
        "embeddings": bell_draw(splits[0], (NCAND, D), 1.0, 6.0, ((0, 256), (1, 2))),
        "factor": draw_factor(jax.random.fold_in(splits[4], 71), 0),
        "residual_diag": jnp.clip(0.5 + 1.0 * jax.random.uniform(splits[2], (NCAND,), jnp.float32) ** block_levels(splits[2], (NCAND,), ((0, 512),), -0.2, 0.2), 0.5, 1.5),
        "pivots": draw_pivots(jax.random.fold_in(splits[4], 71), 0),
    }


ridge_weight = 2.0

def block_columns(embeddings, row_norms, current, chosen_ids):
    chosen = embeddings[chosen_ids]
    chosen_norms = row_norms[chosen_ids]
    dot_panel = jnp.dot(embeddings.astype(jnp.float32), chosen.T.astype(jnp.float32), preferred_element_type=jnp.float32)
    kernel_panel = jnp.exp(-(row_norms[:, None] + chosen_norms[None, :] - 2.0 * dot_panel) / (2.0 * D))
    row_ids = jnp.arange(embeddings.shape[0], dtype=jnp.int32)
    kernel_panel = kernel_panel + ridge_weight * (row_ids[:, None] == chosen_ids[None, :]).astype(jnp.float32)
    kernel_panel = kernel_panel - jnp.dot(current.astype(jnp.float32), current[chosen_ids].T.astype(jnp.float32), precision=lax.Precision.HIGHEST, preferred_element_type=jnp.float32)
    chol_lower = jnp.linalg.cholesky(kernel_panel[chosen_ids])
    return jax.scipy.linalg.solve_triangular(chol_lower, kernel_panel.T, lower=True).T

def reference(embeddings, factor, residual_diag, pivots):
    wide_rows = embeddings.astype(jnp.float32)
    row_norms = jnp.sum(wide_rows * wide_rows, axis=1)
    current = factor
    fresh_list = []
    for block_id in range(2):
        fresh_cols = block_columns(embeddings, row_norms, current, pivots[block_id].astype(jnp.int32))
        fresh_list.append(fresh_cols)
        current = jnp.concatenate([current, fresh_cols], axis=1)
    removed = jnp.sum(fresh_list[0] * fresh_list[0], axis=1) + jnp.sum(fresh_list[1] * fresh_list[1], axis=1)
    return (jnp.stack(fresh_list), residual_diag - removed)
```

```python
import functools

import jax
import jax.numpy as jnp
from jax import lax
from jax.experimental import pallas as pl
from jax.experimental.pallas import tpu as pltpu
from jax.sharding import PartitionSpec as P

F32 = jnp.float32
BF16 = jnp.bfloat16
ridge_weight = 2.0
TILE = 128
SUB = 8


def dot(a, b, dims):
    return lax.dot_general(a, b, (dims, ((), ())), preferred_element_type=F32)


NN = ((1,), (0,))
NT = ((1,), (1,))
TN = ((0,), (0,))


def split2(x):
    hi = x.astype(BF16)
    return hi, (x - hi.astype(F32)).astype(BF16)


def dot3(a, b, dims):
    return dot(a[0], b[0], dims) + (dot(a[0], b[1], dims) + dot(a[1], b[0], dims))


def norm_lanes(rows, first):
    wide = rows.astype(F32)
    neg = jnp.sum(wide * wide, axis=1, keepdims=True) * -0.5
    hi = neg.astype(BF16).astype(F32)
    mid = (neg - hi).astype(BF16).astype(F32)
    low = (neg - hi) - mid
    lane = lax.broadcasted_iota(jnp.int32, (rows.shape[0], TILE), 1)
    at = 0 if first else 3
    out = jnp.where(lane < 6, 1.0, 0.0)
    out = jnp.where(lane == at, hi, out)
    out = jnp.where(lane == at + 1, mid, out)
    out = jnp.where(lane == at + 2, low, out)
    return out.astype(BF16)


def factor_tile(s_ref, cb_ref, pb_ref):
    count = TILE // SUB
    shape = (SUB, TILE)
    lane = lax.broadcasted_iota(jnp.int32, shape, 1)

    def rows(i):
        return s_ref[SUB * i : SUB * (i + 1), :]

    def lane_copy(x, at):
        return jnp.broadcast_to(x[:, at : at + 1], shape)

    def row_copy(ref, at):
        return jnp.broadcast_to(ref[at : at + 1, :], shape)

    ahead = [lane_copy(rows(0), j) for j in range(SUB)]
    for k in range(count):
        base = SUB * k
        diag = (lane >= base) & (lane < base + SUB)
        for j in range(SUB):
            cb_ref[SUB * j : SUB * (j + 1), :] = ahead[j]
        a = [[row_copy(cb_ref, SUB * q + m) if q <= m else None for q in range(SUB)] for m in range(SUB)]
        raw = {}
        for i in range(k + 1, count):
            block = rows(i)
            raw[i] = [lane_copy(block, base + j) for j in range(SUB)]
        near = {i: list(raw[i]) for i in range(k + 1, min(k + 3, count))}
        r = [jnp.where(diag, jnp.where(lane == base + j, 1.0, 0.0), row_copy(s_ref, base + j)) for j in range(SUB)]
        if k + 1 < count:
            block = rows(k + 1)
            ahead = [lane_copy(block, base + SUB + j) for j in range(SUB)]
        inv = []
        low = [[None] * SUB for _ in range(SUB)]
        for j in range(SUB):
            inv.append(lax.rsqrt(a[j][j]))
            for m in range(j + 1, SUB):
                low[m][j] = a[m][j] * inv[j]
            for q in range(j + 1, SUB):
                for m in range(q, SUB):
                    a[m][q] = a[m][q] - low[m][j] * low[q][j]
            for i in near:
                near[i][j] = near[i][j] * inv[j]
                for m in range(j + 1, SUB):
                    near[i][m] = near[i][m] - near[i][j] * low[m][j]
            if k + 1 < count:
                at = SUB * j
                pb_ref[at : at + SUB, :] = near[k + 1][j]
                for m in range(SUB):
                    ahead[m] = ahead[m] - near[k + 1][j] * row_copy(pb_ref, at + m)
            r[j] = r[j] * inv[j]
            for m in range(j + 1, SUB):
                r[m] = r[m] - low[m][j] * r[j]
        for j in range(SUB):
            s_ref[base + j : base + j + 1, :] = r[j][0:1, :]
        if k + 3 < count:
            z = list(r)
            for j in range(SUB - 1, -1, -1):
                z[j] = z[j] * inv[j]
                for m in range(j):
                    z[m] = z[m] - low[j][m] * z[j]
        for i in range(k + 1, count):
            left, right = (near[i], r) if i in near else (raw[i], z)
            total = jnp.where(diag, 0.0, rows(i))
            for j in range(SUB):
                total = total - left[j] * right[j]
            s_ref[SUB * i : SUB * (i + 1), :] = total


def extend(base_ref, piv_ref, pe, pf, eo, fo, res_ref, out_ref, ro_ref, t_ref, q_ref, s_ref, cb_ref, pb_ref, sq_ref):
    width = pe.shape[0]
    own = eo.shape[0]
    scale = 1.0 / pe.shape[1]
    pivot_lanes = norm_lanes(pe[...], False)
    pf_split = split2(pf[...])
    for start in range(0, width, TILE):
        part = slice(start, start + TILE)
        expo = dot(pe[part, :], pe[...], NT) + dot(norm_lanes(pe[part, :], True), pivot_lanes, NT)
        row = start + lax.broadcasted_iota(jnp.int32, (TILE, width), 0)
        col = lax.broadcasted_iota(jnp.int32, (TILE, width), 1)
        value = jnp.exp(expo * scale) + jnp.where(row == col, ridge_weight, 0.0)
        t_ref[part, :] = value - dot3(split2(pf[part, :]), pf_split, NT)
    for start in range(0, own, TILE):
        part = slice(start, start + TILE)
        expo = dot(eo[part, :], pe[...], NT) + dot(norm_lanes(eo[part, :], True), pivot_lanes, NT)
        row = base_ref[0] + start + lax.broadcasted_iota(jnp.int32, (TILE, width), 0)
        value = jnp.exp(expo * scale) + jnp.where(row == piv_ref[...], ridge_weight, 0.0)
        q_ref[part, :] = value - dot3(split2(fo[part, :]), pf_split, NT)
    sq_ref[...] = jnp.zeros_like(sq_ref)
    count = width // TILE

    def outer(block, carry):
        at = pl.multiple_of(block * TILE, TILE)
        here = pl.ds(at, TILE)
        s_ref[...] = t_ref[here, here]
        factor_tile(s_ref, cb_ref, pb_ref)
        tall = lax.broadcasted_iota(jnp.int32, (TILE, TILE), 0)
        wide = lax.broadcasted_iota(jnp.int32, (TILE, TILE), 1)
        inverse = split2(jnp.where(wide <= tall, s_ref[...], 0.0))
        upper = split2(dot3(inverse, split2(t_ref[here, :]), NN))
        t_ref[...] -= dot3(upper, upper, TN)
        fresh = dot3(split2(q_ref[:, here]), inverse, NT)
        half = lax.rem(block, count // 2)
        out_ref[block // (count // 2), :, pl.ds(pl.multiple_of(half * TILE, TILE), TILE)] = fresh
        sq_ref[...] += fresh * fresh
        q_ref[...] -= dot3(split2(fresh), upper, NN)
        return carry

    lax.fori_loop(0, count, outer, 0)
    hi, low = split2(sq_ref[...])
    ones = jnp.ones((SUB, TILE), BF16)
    removed = dot(ones, hi, NT) + dot(ones, low, NT)
    ro_ref[...] = res_ref[...] - removed[0:1, :]


def extend_call(base, pivots, pe, pf, eo, fo, residual, interpret=False):
    width, depth = pe.shape
    own, rank = fo.shape
    vmem = pl.BlockSpec(memory_space=pltpu.VMEM)
    return pl.pallas_call(
        extend,
        out_shape=(
            jax.ShapeDtypeStruct((2, own, width // 2), F32),
            jax.ShapeDtypeStruct((1, own), F32),
        ),
        in_specs=[pl.BlockSpec(memory_space=pltpu.SMEM)] + [vmem] * 6,
        out_specs=(vmem, vmem),
        scratch_shapes=[
            pltpu.VMEM((width, width), F32),
            pltpu.VMEM((own, width), F32),
            pltpu.VMEM((TILE, TILE), F32),
            pltpu.VMEM((SUB * SUB, TILE), F32),
            pltpu.VMEM((SUB * SUB, TILE), F32),
            pltpu.VMEM((own, TILE), F32),
        ],
        compiler_params=pltpu.CompilerParams(vmem_limit_bytes=40 * 1024 * 1024),
        name="extend",
        interpret=interpret,
    )(base, pivots, pe, pf, eo, fo, residual)


def shards(embeddings, factor, residual_diag, pivots):
    local_rows, feat_cols = embeddings.shape
    half_rows = factor.shape[0]
    row_group = lax.axis_index("rows")
    feat_group = lax.axis_index("feat")
    rows_start = row_group * local_rows
    half_start = rows_start + feat_group * half_rows
    flat = pivots.reshape(-1)
    owner = flat // local_rows
    prev = jnp.concatenate([jnp.full((2, 1), -1, jnp.int32), owner.reshape(2, -1)[:, :-1]], axis=1).reshape(-1)
    rank = (owner == prev).astype(jnp.int32)
    block_of = jnp.arange(flat.shape[0]) // pivots.shape[1]
    slot = block_of * 2 + rank
    mine = (owner == row_group)
    slot_id = jnp.sum(jnp.where(mine[None, :] & (slot[None, :] == jnp.arange(4)[:, None]), flat[None, :] + 1, 0), axis=1) - 1
    off = slot_id - rows_start
    have = slot_id >= 0
    emb = jnp.where(have[:, None], jnp.take(embeddings, jnp.clip(off, 0, local_rows - 1), axis=0), 0)
    hoff = off - feat_group * half_rows
    hhave = have & (hoff >= 0) & (hoff < half_rows)
    fac = jnp.where(hhave[:, None], jnp.take(factor, jnp.clip(hoff, 0, half_rows - 1), axis=0), 0)
    slots = jnp.concatenate([emb.astype(F32), fac], axis=1)
    every = lax.all_gather(slots, ("rows", "feat"))
    every = every.reshape(-1, 2, 4, slots.shape[1])
    cols = jnp.concatenate([every[:, 0, :, :feat_cols], every[:, 1, :, :feat_cols], every[:, 0, :, feat_cols:] + every[:, 1, :, feat_cols:]], axis=-1).reshape(-1, 2 * feat_cols + 256)
    hot = ((owner * 4 + slot)[:, None] == jnp.arange(cols.shape[0])[None, :]).astype(F32)
    picked = jnp.dot(hot, cols, precision=lax.Precision.HIGHEST)
    pe = picked[:, : 2 * feat_cols].astype(BF16)
    pf = picked[:, 2 * feat_cols :]
    eo = lax.all_to_all(embeddings, "feat", 0, 1, tiled=True)
    base = half_start.reshape(1).astype(jnp.int32)
    fresh, removed = extend_call(base, flat.reshape(1, -1), pe, pf, eo, factor, residual_diag.reshape(1, -1))
    return fresh, removed.reshape(-1)


def solution(mesh):
    return jax.shard_map(
        shards,
        mesh=mesh,
        in_specs=(P("rows", "feat"), P(("rows", "feat"), None), P(("rows", "feat")), P()),
        out_specs=(P(None, ("rows", "feat"), None), P(("rows", "feat"))),
        check_vma=False,
    )
```

```python
import functools

import jax
import jax.numpy as jnp
from jax import lax
from jax.experimental import pallas as pl
from jax.experimental.pallas import tpu as pltpu
from jax.sharding import PartitionSpec as P

F32 = jnp.float32
BF16 = jnp.bfloat16
ridge_weight = 2.0
TILE = 128
CAP = 2
X_SIDE = 4
SIDE = 8
MESH = pl.DeviceIdType.MESH
SUB = 8


def dot(a, b, dims):
    return lax.dot_general(a, b, (dims, ((), ())), preferred_element_type=F32)


NN = ((1,), (0,))
NT = ((1,), (1,))
TN = ((0,), (0,))


def split2(x):
    hi = x.astype(BF16)
    return hi, (x - hi.astype(F32)).astype(BF16)


def dot3(a, b, dims):
    return dot(a[0], b[0], dims) + (dot(a[0], b[1], dims) + dot(a[1], b[0], dims))


def norm_lanes(neg, first):
    hi = neg.astype(BF16).astype(F32)
    mid = (neg - hi).astype(BF16).astype(F32)
    low = (neg - hi) - mid
    lane = lax.broadcasted_iota(jnp.int32, (neg.shape[0], TILE), 1)
    at = 0 if first else 3
    out = jnp.where(lane < 6, 1.0, 0.0)
    out = jnp.where(lane == at, hi, out)
    out = jnp.where(lane == at + 1, mid, out)
    out = jnp.where(lane == at + 2, low, out)
    return out.astype(BF16)


def factor_tile(s_ref, cb_ref, pb_ref):
    count = TILE // SUB
    shape = (SUB, TILE)
    lane = lax.broadcasted_iota(jnp.int32, shape, 1)

    def rows(i):
        return s_ref[SUB * i : SUB * (i + 1), :]

    def lane_copy(x, at):
        return jnp.broadcast_to(x[:, at : at + 1], shape)

    def row_copy(ref, at):
        return jnp.broadcast_to(ref[at : at + 1, :], shape)

    ahead = [lane_copy(rows(0), j) for j in range(SUB)]
    for k in range(count):
        base = SUB * k
        diag = (lane >= base) & (lane < base + SUB)
        for j in range(SUB):
            cb_ref[SUB * j : SUB * (j + 1), :] = ahead[j]
        a = [[row_copy(cb_ref, SUB * q + m) if q <= m else None for q in range(SUB)] for m in range(SUB)]
        raw = {}
        for i in range(k + 1, count):
            block = rows(i)
            raw[i] = [lane_copy(block, base + j) for j in range(SUB)]
        near = {i: list(raw[i]) for i in range(k + 1, min(k + 3, count))}
        r = [jnp.where(diag, jnp.where(lane == base + j, 1.0, 0.0), row_copy(s_ref, base + j)) for j in range(SUB)]
        if k + 1 < count:
            block = rows(k + 1)
            ahead = [lane_copy(block, base + SUB + j) for j in range(SUB)]
        inv = []
        low = [[None] * SUB for _ in range(SUB)]
        for j in range(SUB):
            inv.append(lax.rsqrt(a[j][j]))
            for m in range(j + 1, SUB):
                low[m][j] = a[m][j] * inv[j]
            for q in range(j + 1, SUB):
                for m in range(q, SUB):
                    a[m][q] = a[m][q] - low[m][j] * low[q][j]
            for i in near:
                near[i][j] = near[i][j] * inv[j]
                for m in range(j + 1, SUB):
                    near[i][m] = near[i][m] - near[i][j] * low[m][j]
            if k + 1 < count:
                at = SUB * j
                pb_ref[at : at + SUB, :] = near[k + 1][j]
                for m in range(SUB):
                    ahead[m] = ahead[m] - near[k + 1][j] * row_copy(pb_ref, at + m)
            r[j] = r[j] * inv[j]
            for m in range(j + 1, SUB):
                r[m] = r[m] - low[m][j] * r[j]
        for j in range(SUB):
            s_ref[base + j : base + j + 1, :] = r[j][0:1, :]
        if k + 3 < count:
            z = list(r)
            for j in range(SUB - 1, -1, -1):
                z[j] = z[j] * inv[j]
                for m in range(j):
                    z[m] = z[m] - low[j][m] * z[j]
        for i in range(k + 1, count):
            left, right = (near[i], r) if i in near else (raw[i], z)
            total = jnp.where(diag, 0.0, rows(i))
            for j in range(SUB):
                total = total - left[j] * right[j]
            s_ref[SUB * i : SUB * (i + 1), :] = total


def places(sides):
    x_side, side = sides
    r = lax.axis_index("rows")
    core = lax.axis_index("feat")
    x = r // (side * side)
    z = lax.rem(r // side, side)
    y = lax.rem(r, side)
    first = z + core * (y - z)
    other = y + core * (z - y)
    first_step = side + core * (1 - side)
    other_step = 1 + core * (side - 1)
    return r, core, x, first, other, first_step, other_step


def gather(sides, emb, fac, piv, a_ref, b_ref, eo_ref, g_ref, h_ref, sx_ref, s1, r1, sc, rc, s2a, r2a, s2b, r2b, s3a, r3a, s3b, r3b, sfa, rfa, sfb, rfb, se, re):
    x_side, side = sides
    r, core, x, first, other, first_step, other_step = places(sides)
    sib = 1 - core
    cols = emb.shape[1]
    half = fac.shape[0]
    rank = fac.shape[1] // 2
    group = 2 * CAP

    def along_first(i):
        return r + (i - first) * first_step

    def along_other(i):
        return r + (i - other) * other_step

    def along_x(i):
        return r + (i - x) * (side * side)

    def turn(at, step, size):
        return lax.rem(at + step, size)

    barrier = pltpu.get_barrier_semaphore()

    def greet(row, at):
        pl.semaphore_signal(barrier, inc=1, device_id=(row, at), device_id_type=MESH)

    greet(r, sib)
    for d in range(1, side):
        greet(along_first(turn(first, d, side)), core)
        greet(along_other(turn(other, d, side)), core)
        greet(along_first(turn(first, d, side)), sib)
        greet(along_other(turn(other, d, side)), sib)
    for d in range(1, x_side):
        greet(along_x(turn(x, d, x_side)), core)

    start = r * emb.shape[0]
    ids = []
    for block in range(2):
        width = piv.shape[1] // 2
        chosen = piv[:, block * width : (block + 1) * width]
        mine = (chosen >= start) & (chosen < start + emb.shape[0])
        least = jnp.min(jnp.where(mine, chosen, 1 << 30), axis=1, keepdims=True)
        most = jnp.max(jnp.where(mine, chosen, -1), axis=1, keepdims=True)
        ids += [least, jnp.where(most == least, -1, most)]

    def picks(count, offset, odd):
        sub = lax.broadcasted_iota(jnp.int32, (2 * SUB, count), 0) - group * odd
        row = lax.broadcasted_iota(jnp.int32, (2 * SUB, count), 1) + offset
        hot = jnp.zeros((2 * SUB, count), F32)
        for s, one in enumerate(ids):
            hot = jnp.where((sub == s) & (row == one), 1.0, hot)
        return hot.astype(BF16)

    odd_first = lax.rem(first, 2)
    odd_other = lax.rem(other, 2)
    half_start = start + core * half
    g_ref[first, :, :cols] = dot(picks(emb.shape[0], start, odd_first), emb[...], NN)[:SUB]
    wide = fac[...]
    top = wide.astype(BF16)
    mid = (wide - top.astype(F32)).astype(BF16)

    def fac_rows(odd):
        hot = picks(half, half_start, odd)
        return (dot(hot, top, NN) + dot(hot, mid, NN))[:SUB]

    here = fac_rows(odd_first)
    there = fac_rows(odd_other)
    low_half = core == 0
    g_ref[first, :, cols:] = jnp.where(low_half, here[:, :rank], here[:, rank:])
    sx_ref[...] = jnp.where(low_half, there[:, rank:], there[:, :rank])

    pl.semaphore_wait(barrier, 4 * (side - 1) + 1 + x_side - 1)

    def copy(src, dst, send, recv, row, at):
        return pltpu.make_async_remote_copy(
            src_ref=src, dst_ref=dst, send_sem=send, recv_sem=recv, device_id=(row, at), device_id_type=MESH
        )

    sends = []

    def go(*args):
        one = copy(*args)
        one.start()
        sends.append(one)

    for d in range(1, side):
        to = along_first(turn(first, d, side))
        go(g_ref.at[first], g_ref.at[first], s1.at[d], r1.at[first], to, core)
    for d in range(side):
        to = along_other(turn(other, d, side))
        go(sx_ref, h_ref.at[other], sc.at[d], rc.at[other], to, sib)
    go(emb.at[pl.ds(pl.multiple_of(sib * half, half), half)], eo_ref, se, re, r, sib)
    for d in range(1, side):
        i = turn(first, d, side)
        copy(g_ref.at[i], g_ref.at[i], s1.at[d], r1.at[i], r, sib).wait_recv()
    for p in range(side // 2):
        rows = slice(SUB * p, SUB * (p + 1))
        both = g_ref[2 * p, :, :cols] + g_ref[2 * p + 1, :, :cols]
        if p % 2 == 0:
            held = both
        else:
            a_ref[0, x, other, SUB * (p - 1) : SUB * (p + 1), :] = jnp.concatenate([held, both], axis=0).astype(BF16)
    for d in range(1, side):
        to = along_other(turn(other, d, side))
        go(a_ref.at[0, x, other], a_ref.at[0, x, other], s2a.at[d], r2a.at[other], to, core)
    for i in range(side):
        copy(sx_ref, h_ref.at[i], sc.at[0], rc.at[i], r, sib).wait_recv()
    for p in range(0, side // 2, 2):
        both = [
            (g_ref[2 * q, :, cols:] + g_ref[2 * q + 1, :, cols:]) + (h_ref[2 * q] + h_ref[2 * q + 1]) for q in (p, p + 1)
        ]
        both = jnp.concatenate(both, axis=0)
        top = both.astype(BF16)
        rows = slice(SUB * p, SUB * (p + 2))
        b_ref[0, other, x, rows, :rank] = top
        b_ref[0, other, x, rows, rank:] = (both - top.astype(F32)).astype(BF16)
    for d in range(1, x_side):
        to = along_x(turn(x, d, x_side))
        go(b_ref.at[0, other, x], b_ref.at[0, other, x], s2b.at[d], r2b.at[x], to, core)

    for d in range(1, side):
        i = turn(other, d, side)
        copy(a_ref.at[0, x, i], a_ref.at[0, x, i], s2a.at[d], r2a.at[i], r, sib).wait_recv()
    for d in range(1, x_side):
        to = along_x(turn(x, d, x_side))
        go(a_ref.at[0, x], a_ref.at[0, x], s3a.at[d], r3a.at[x], to, core)
    for d in range(1, x_side):
        i = turn(x, d, x_side)
        copy(b_ref.at[0, other, i], b_ref.at[0, other, i], s2b.at[d], r2b.at[i], r, sib).wait_recv()
    for d in range(1, side):
        to = along_other(turn(other, d, side))
        go(b_ref.at[0, other], b_ref.at[0, other], s3b.at[d], r3b.at[other], to, core)

    go(a_ref.at[0, x], a_ref.at[1, x], sfa.at[0], rfa.at[x], r, sib)
    go(b_ref.at[0, other], b_ref.at[1, other], sfb.at[0], rfb.at[other], r, sib)
    for d in range(1, side):
        i = turn(other, d, side)
        copy(b_ref.at[0, i], b_ref.at[0, i], s3b.at[d], r3b.at[i], r, sib).wait_recv()
        go(b_ref.at[0, i], b_ref.at[1, i], sfb.at[d], rfb.at[i], r, sib)
    for d in range(1, x_side):
        i = turn(x, d, x_side)
        copy(a_ref.at[0, i], a_ref.at[0, i], s3a.at[d], r3a.at[i], r, sib).wait_recv()
        go(a_ref.at[0, i], a_ref.at[1, i], sfa.at[d], rfa.at[i], r, sib)
    for i in range(side):
        copy(b_ref.at[0, i], b_ref.at[1, i], sfb.at[i], rfb.at[i], r, sib).wait_recv()
    for i in range(x_side):
        copy(a_ref.at[0, i], a_ref.at[1, i], sfa.at[i], rfa.at[i], r, sib).wait_recv()
    copy(eo_ref, eo_ref, se, re, r, sib).wait_recv()
    for one in sends:
        one.wait_send()


def gather_call(emb, fac, piv, sides=(X_SIDE, SIDE)):
    x_side, side = sides
    vmem = pl.BlockSpec(memory_space=pltpu.VMEM)
    group = side * 2 * CAP
    cols, rank = emb.shape[1], fac.shape[1]
    dma = pltpu.SemaphoreType.DMA
    counts = [side, side, side, side, side, side, x_side, x_side, x_side, x_side, side, side, x_side, x_side, side, side]
    return pl.pallas_call(
        functools.partial(gather, sides),
        out_shape=(
            jax.ShapeDtypeStruct((2, x_side, side, group, cols), BF16),
            jax.ShapeDtypeStruct((2, side, x_side, group, rank), BF16),
            jax.ShapeDtypeStruct((fac.shape[0], cols), BF16),
        ),
        in_specs=[vmem] * 3,
        out_specs=(vmem,) * 3,
        scratch_shapes=[
            pltpu.VMEM((side, SUB, cols + rank // 2), F32),
            pltpu.VMEM((side, SUB, rank // 2), F32),
            pltpu.VMEM((SUB, rank // 2), F32),
        ]
        + [dma((n,)) for n in counts]
        + [dma, dma],
        compiler_params=pltpu.CompilerParams(
            collective_id=0, has_side_effects=True, vmem_limit_bytes=32 * 1024 * 1024
        ),
        name="gather_pivots",
    )(emb, fac, piv)


def slot_rows(piv, local_rows, sides, core, part_x_first):
    x_side, side = sides
    width = piv.shape[1]
    owner = ((piv.astype(F32) + 0.5) * (1.0 / local_rows)).astype(jnp.int32)
    lane = lax.broadcasted_iota(jnp.int32, piv.shape, 1)
    second = lane >= width // 2
    before = pltpu.roll(jnp.broadcast_to(owner, (SUB, width)), 1, axis=1)[0:1, :]
    again = (before == owner) & (lane != 0) & (lane != width // 2)
    slot = jnp.where(second, CAP, 0) + jnp.where(again, 1, 0)
    bits = side.bit_length() - 1
    y = owner & (side - 1)
    z = (owner >> bits) & (side - 1)
    x = owner >> (2 * bits)
    first = jnp.where(core == 0, z, y)
    other = jnp.where(core == 0, y, z)
    outer = x * side + other if part_x_first else other * x_side + x
    flat = ((outer * side + first) * (2 * CAP) + slot).astype(F32)
    tiles = [
        jnp.transpose(jnp.broadcast_to(flat[:, at : at + TILE], (TILE, TILE))) for at in range(0, width, TILE)
    ]
    return tiles


def pick_rows(src, tiles, dst):
    count = src.shape[0]
    data = src[...]
    for t, tile in enumerate(tiles):
        lane = lax.broadcasted_iota(jnp.int32, (TILE, TILE), 1).astype(F32)
        hot = jnp.concatenate(
            [jnp.where(tile == lane + float(at), 1.0, 0.0).astype(BF16) for at in range(0, count, TILE)], axis=1
        )
        dst[t * TILE : (t + 1) * TILE, :] = dot(hot, data, NN).astype(BF16)


def extend(sides, base_ref, piv_ref, a_ref, b_ref, emb, es, fo, res_ref, out_ref, ro_ref, pe, ps, pf, fs, t_ref, q_ref, s_ref, cb_ref, pb_ref, sq_ref):
    core = base_ref[1]
    width = pe.shape[0]
    own = es.shape[0]
    cols = es.shape[1]
    rank = fo.shape[1]
    scale = 1.0 / (2 * cols)
    for at, at_core, emb_out, fac_out in ((0, core, pe, pf), (1, 1 - core, ps, fs)):
        pick_rows(a_ref.at[at], slot_rows(piv_ref[...], emb.shape[0], sides, at_core, True), emb_out)
        pick_rows(b_ref.at[at], slot_rows(piv_ref[...], emb.shape[0], sides, at_core, False), fac_out)

    def norms(one, two):
        one, two = one.astype(F32), two.astype(F32)
        return jnp.sum(one * one + two * two, axis=1, keepdims=True) * -0.5

    def fac_dot(left, right):
        h = rank // 2
        lhs = jnp.concatenate([left[0], left[0], left[1]], axis=1)
        return dot(lhs, right, NT)

    h = rank // 2
    right = jnp.concatenate(
        [pf[:, :h], fs[:, :h], pf[:, h:], fs[:, h:], pf[:, :h], fs[:, :h]], axis=1
    )
    pivot_lanes = norm_lanes(norms(pe[...], ps[...]), False)
    for start in range(0, width, TILE):
        part = slice(start, start + TILE)
        expo = dot(pe[part, :], pe[...], NT) + dot(ps[part, :], ps[...], NT)
        expo += dot(norm_lanes(norms(pe[part, :], ps[part, :]), True), pivot_lanes, NT)
        row = start + lax.broadcasted_iota(jnp.int32, (TILE, width), 0)
        col = lax.broadcasted_iota(jnp.int32, (TILE, width), 1)
        value = jnp.exp(expo * scale) + jnp.where(row == col, ridge_weight, 0.0)
        high = jnp.concatenate([pf[part, :h], fs[part, :h]], axis=1)
        low = jnp.concatenate([pf[part, h:], fs[part, h:]], axis=1)
        t_ref[part, :] = value - fac_dot((high, low), right)
    for start in range(0, own, TILE):
        part = slice(start, start + TILE)
        mine = emb[pl.ds(pl.multiple_of(core * own + start, TILE), TILE), :]
        expo = dot(mine, pe[...], NT) + dot(es[part, :], ps[...], NT)
        expo += dot(norm_lanes(norms(mine, es[part, :]), True), pivot_lanes, NT)
        row = base_ref[0] + start + lax.broadcasted_iota(jnp.int32, (TILE, width), 0)
        value = jnp.exp(expo * scale) + jnp.where(row == piv_ref[...], ridge_weight, 0.0)
        near = fo[part, pl.ds(pl.multiple_of(core * h, h), h)]
        far = fo[part, pl.ds(pl.multiple_of((1 - core) * h, h), h)]
        q_ref[part, :] = value - fac_dot(split2(jnp.concatenate([near, far], axis=1)), right)
    sq_ref[...] = jnp.zeros_like(sq_ref)
    count = width // TILE

    def outer(block, carry):
        at = pl.multiple_of(block * TILE, TILE)
        here = pl.ds(at, TILE)
        s_ref[...] = t_ref[here, here]
        factor_tile(s_ref, cb_ref, pb_ref)
        tall = lax.broadcasted_iota(jnp.int32, (TILE, TILE), 0)
        wide = lax.broadcasted_iota(jnp.int32, (TILE, TILE), 1)
        inverse = split2(jnp.where(wide <= tall, s_ref[...], 0.0))
        upper = split2(dot3(inverse, split2(t_ref[here, :]), NN))
        t_ref[...] -= dot3(upper, upper, TN)
        fresh = dot3(split2(q_ref[:, here]), inverse, NT)
        half = lax.rem(block, count // 2)
        out_ref[block // (count // 2), :, pl.ds(pl.multiple_of(half * TILE, TILE), TILE)] = fresh
        sq_ref[...] += fresh * fresh
        q_ref[...] -= dot3(split2(fresh), upper, NN)
        return carry

    lax.fori_loop(0, count, outer, 0)
    hi, low = split2(sq_ref[...])
    ones = jnp.ones((SUB, TILE), BF16)
    removed = dot(ones, hi, NT) + dot(ones, low, NT)
    ro_ref[...] = res_ref[...] - removed[0:1, :]


def extend_call(base, pivots, a, b, emb, es, fo, residual, sides=(X_SIDE, SIDE)):
    width = pivots.shape[1]
    own, rank = fo.shape
    cols = emb.shape[1]
    vmem = pl.BlockSpec(memory_space=pltpu.VMEM)
    return pl.pallas_call(
        functools.partial(extend, sides),
        out_shape=(
            jax.ShapeDtypeStruct((2, own, width // 2), F32),
            jax.ShapeDtypeStruct((1, own), F32),
        ),
        in_specs=[pl.BlockSpec(memory_space=pltpu.SMEM)] + [vmem] * 7,
        out_specs=(vmem, vmem),
        scratch_shapes=[
            pltpu.VMEM((width, cols), BF16),
            pltpu.VMEM((width, cols), BF16),
            pltpu.VMEM((width, rank), BF16),
            pltpu.VMEM((width, rank), BF16),
            pltpu.VMEM((width, width), F32),
            pltpu.VMEM((own, width), F32),
            pltpu.VMEM((TILE, TILE), F32),
            pltpu.VMEM((SUB * SUB, TILE), F32),
            pltpu.VMEM((SUB * SUB, TILE), F32),
            pltpu.VMEM((own, TILE), F32),
        ],
        compiler_params=pltpu.CompilerParams(vmem_limit_bytes=40 * 1024 * 1024),
        name="extend",
    )(base, pivots, a, b, emb, es, fo, residual)


def shards(sides, embeddings, factor, residual_diag, pivots):
    local_rows = embeddings.shape[0]
    half_rows, rank = factor.shape
    core = lax.axis_index("feat")
    base = lax.axis_index("rows") * local_rows + core * half_rows
    flat = pivots.reshape(1, -1)
    a, b, es = gather_call(embeddings, factor, flat, sides)
    a = a.reshape(2, -1, embeddings.shape[1])
    b = b.reshape(2, -1, rank)
    place = jnp.stack([base, core]).astype(jnp.int32)
    fresh, removed = extend_call(place, flat, a, b, embeddings, es, factor, residual_diag.reshape(1, -1), sides)
    return fresh, removed.reshape(-1)


def solution(mesh):
    return jax.shard_map(
        functools.partial(shards, (X_SIDE, SIDE)),
        mesh=mesh,
        in_specs=(P("rows", "feat"), P(("rows", "feat"), None), P(("rows", "feat")), P()),
        out_specs=(P(None, ("rows", "feat"), None), P(("rows", "feat"))),
        check_vma=False,
    )
```

```python
import functools

import jax
import jax.numpy as jnp
from jax import lax
from jax.experimental import pallas as pl
from jax.experimental.pallas import tpu as pltpu
from jax.sharding import PartitionSpec as P

F32 = jnp.float32
BF16 = jnp.bfloat16
ridge_weight = 2.0
TILE = 128
CAP = 2
X_SIDE = 4
SIDE = 8
FAC_MAX = 0.1
LEVELS = 32767.0
MESH = pl.DeviceIdType.MESH
SUB = 8


def dot(a, b, dims):
    return lax.dot_general(a, b, (dims, ((), ())), preferred_element_type=F32)


NN = ((1,), (0,))
NT = ((1,), (1,))
TN = ((0,), (0,))


def split2(x):
    hi = x.astype(BF16)
    return hi, (x - hi.astype(F32)).astype(BF16)


def dot3(a, b, dims):
    return dot(a[0], b[0], dims) + (dot(a[0], b[1], dims) + dot(a[1], b[0], dims))


def norm_lanes(neg, first):
    hi = neg.astype(BF16).astype(F32)
    mid = (neg - hi).astype(BF16).astype(F32)
    low = (neg - hi) - mid
    lane = lax.broadcasted_iota(jnp.int32, (neg.shape[0], TILE), 1)
    at = 0 if first else 3
    out = jnp.where(lane < 6, 1.0, 0.0)
    out = jnp.where(lane == at, hi, out)
    out = jnp.where(lane == at + 1, mid, out)
    out = jnp.where(lane == at + 2, low, out)
    return out.astype(BF16)


def factor_tile(s_ref, cb_ref, pb_ref):
    count = TILE // SUB
    shape = (SUB, TILE)
    lane = lax.broadcasted_iota(jnp.int32, shape, 1)

    def rows(i):
        return s_ref[SUB * i : SUB * (i + 1), :]

    def lane_copy(x, at):
        return jnp.broadcast_to(x[:, at : at + 1], shape)

    def row_copy(ref, at):
        return jnp.broadcast_to(ref[at : at + 1, :], shape)

    ahead = [lane_copy(rows(0), j) for j in range(SUB)]
    for k in range(count):
        base = SUB * k
        diag = (lane >= base) & (lane < base + SUB)
        for j in range(SUB):
            cb_ref[SUB * j : SUB * (j + 1), :] = ahead[j]
        a = [[row_copy(cb_ref, SUB * q + m) if q <= m else None for q in range(SUB)] for m in range(SUB)]
        raw = {}
        for i in range(k + 1, count):
            block = rows(i)
            raw[i] = [lane_copy(block, base + j) for j in range(SUB)]
        near = {i: list(raw[i]) for i in range(k + 1, min(k + 3, count))}
        r = [jnp.where(diag, jnp.where(lane == base + j, 1.0, 0.0), row_copy(s_ref, base + j)) for j in range(SUB)]
        if k + 1 < count:
            block = rows(k + 1)
            ahead = [lane_copy(block, base + SUB + j) for j in range(SUB)]
        inv = []
        low = [[None] * SUB for _ in range(SUB)]
        for j in range(SUB):
            inv.append(lax.rsqrt(a[j][j]))
            for m in range(j + 1, SUB):
                low[m][j] = a[m][j] * inv[j]
            for q in range(j + 1, SUB):
                for m in range(q, SUB):
                    a[m][q] = a[m][q] - low[m][j] * low[q][j]
            for i in near:
                near[i][j] = near[i][j] * inv[j]
                for m in range(j + 1, SUB):
                    near[i][m] = near[i][m] - near[i][j] * low[m][j]
            if k + 1 < count:
                at = SUB * j
                pb_ref[at : at + SUB, :] = near[k + 1][j]
                for m in range(SUB):
                    ahead[m] = ahead[m] - near[k + 1][j] * row_copy(pb_ref, at + m)
            r[j] = r[j] * inv[j]
            for m in range(j + 1, SUB):
                r[m] = r[m] - low[m][j] * r[j]
        for j in range(SUB):
            s_ref[base + j : base + j + 1, :] = r[j][0:1, :]
        if k + 3 < count:
            z = list(r)
            for j in range(SUB - 1, -1, -1):
                z[j] = z[j] * inv[j]
                for m in range(j):
                    z[m] = z[m] - low[j][m] * z[j]
        for i in range(k + 1, count):
            left, right = (near[i], r) if i in near else (raw[i], z)
            total = jnp.where(diag, 0.0, rows(i))
            for j in range(SUB):
                total = total - left[j] * right[j]
            s_ref[SUB * i : SUB * (i + 1), :] = total


def places(sides):
    x_side, side = sides
    r = lax.axis_index("rows")
    core = lax.axis_index("feat")
    x = r // (side * side)
    z = lax.rem(r // side, side)
    y = lax.rem(r, side)
    first = z + core * (y - z)
    other = y + core * (z - y)
    first_step = side + core * (1 - side)
    other_step = 1 + core * (side - 1)
    return r, core, x, first, other, first_step, other_step


def gather(sides, emb_any, fac_any, piv, a_ref, b_ref, eo_ref, emb, fac, g_ref, s1, r1, s2a, r2a, s2b, r2b, s3a, r3a, s3b, r3b, sfa, rfa, sfb, rfb, se, re, le, lf):
    x_side, side = sides
    r, core, x, first, other, first_step, other_step = places(sides)
    sib = 1 - core
    cols = emb.shape[1]
    half = fac.shape[0]
    group = 2 * CAP

    load_emb = pltpu.make_async_copy(emb_any, emb, le)
    load_fac = pltpu.make_async_copy(fac_any, fac, lf)
    load_emb.start()
    load_fac.start()

    def along_first(i):
        return r + (i - first) * first_step

    def along_other(i):
        return r + (i - other) * other_step

    def along_x(i):
        return r + (i - x) * (side * side)

    def turn(at, step, size):
        return lax.rem(at + step, size)

    barrier = pltpu.get_barrier_semaphore()

    def greet(row, at):
        pl.semaphore_signal(barrier, inc=1, device_id=(row, at), device_id_type=MESH)

    greet(r, sib)
    for d in range(1, side):
        greet(along_first(turn(first, d, side)), core)
        greet(along_other(turn(other, d, side)), core)
    for d in range(1, x_side):
        greet(along_x(turn(x, d, x_side)), core)

    start = r * emb.shape[0]
    ids = []
    for block in range(2):
        chosen = piv[block : block + 1, :]
        mine = (chosen >= start) & (chosen < start + emb.shape[0])
        least = jnp.min(jnp.where(mine, chosen, 1 << 30), axis=1, keepdims=True)
        most = jnp.max(jnp.where(mine, chosen, -1), axis=1, keepdims=True)
        ids += [least, jnp.where(most == least, -1, most)]

    def picks(count, offset):
        sub = lax.broadcasted_iota(jnp.int32, (2 * SUB, count), 0)
        row = lax.broadcasted_iota(jnp.int32, (2 * SUB, count), 1) + offset
        hot = jnp.zeros((2 * SUB, count), F32)
        for s, one in enumerate(ids):
            hot = jnp.where((sub == s) & (row == one), 1.0, hot)
        return hot.astype(BF16)

    hot_fac = picks(half, start + core * half)
    hot_emb = picks(emb.shape[0], start)
    load_emb.wait()
    g_ref[first, :, :cols] = dot(hot_emb, emb[...], NN)[:SUB]
    load_fac.wait()
    top, mid = split2(fac[...])
    own_fac = (dot(hot_fac, top, NN) + dot(hot_fac, mid, NN))[:SUB] * (LEVELS / FAC_MAX)
    own_fac = jnp.floor(own_fac + 0.5)
    g_ref[first, :, cols:] = jnp.clip(own_fac, -LEVELS, LEVELS)

    pl.semaphore_wait(barrier, 2 * (side - 1) + x_side)

    def copy(src, dst, send, recv, row, at):
        return pltpu.make_async_remote_copy(
            src_ref=src, dst_ref=dst, send_sem=send, recv_sem=recv, device_id=(row, at), device_id_type=MESH
        )

    sends = []

    def go(*args):
        one = copy(*args)
        one.start()
        sends.append(one)

    for d in range(1, side):
        to = along_first(turn(first, d, side))
        go(g_ref.at[first], g_ref.at[first], s1.at[d], r1.at[first], to, core)
    go(emb.at[pl.ds(pl.multiple_of(sib * half, half), half)], eo_ref, se, re, r, sib)
    to_row = lax.broadcasted_iota(jnp.int32, (group * side, SUB * side), 0)
    from_row = lax.broadcasted_iota(jnp.int32, (group * side, SUB * side), 1)
    half_rows = CAP * side
    block = jnp.where(to_row >= half_rows, 1, 0)
    inside = to_row - block * half_rows
    source = (inside >> 1) * SUB + block * CAP + (inside & 1)
    order = jnp.where(from_row == source, 1.0, 0.0).astype(BF16)
    for d in range(1, side):
        i = turn(first, d, side)
        copy(g_ref.at[i], g_ref.at[i], s1.at[d], r1.at[i], r, sib).wait_recv()
    held = g_ref[...].reshape(SUB * side, -1)
    a_ref[0, x, other] = dot(order, held[:, :cols].astype(BF16), NN).astype(BF16)
    for d in range(1, side):
        to = along_other(turn(other, d, side))
        go(a_ref.at[0, x, other], a_ref.at[0, x, other], s2a.at[d], r2a.at[other], to, core)
    top, mid = split2(held[:, cols:])
    ints = dot(order, top, NN) + dot(order, mid, NN)
    b_ref[0, other, x] = ints.astype(jnp.int32).astype(jnp.int16)
    for d in range(1, x_side):
        to = along_x(turn(x, d, x_side))
        go(b_ref.at[0, other, x], b_ref.at[0, other, x], s2b.at[d], r2b.at[x], to, core)

    for d in range(1, side):
        i = turn(other, d, side)
        copy(a_ref.at[0, x, i], a_ref.at[0, x, i], s2a.at[d], r2a.at[i], r, sib).wait_recv()
    for d in range(1, x_side):
        to = along_x(turn(x, d, x_side))
        go(a_ref.at[0, x], a_ref.at[0, x], s3a.at[d], r3a.at[x], to, core)
    for d in range(1, x_side):
        i = turn(x, d, x_side)
        copy(b_ref.at[0, other, i], b_ref.at[0, other, i], s2b.at[d], r2b.at[i], r, sib).wait_recv()
    for d in range(1, side):
        to = along_other(turn(other, d, side))
        go(b_ref.at[0, other], b_ref.at[0, other], s3b.at[d], r3b.at[other], to, core)

    go(a_ref.at[0, x], a_ref.at[1, x], sfa.at[0], rfa.at[x], r, sib)
    go(b_ref.at[0, other], b_ref.at[1, other], sfb.at[0], rfb.at[other], r, sib)
    for d in range(1, side):
        i = turn(other, d, side)
        copy(b_ref.at[0, i], b_ref.at[0, i], s3b.at[d], r3b.at[i], r, sib).wait_recv()
        go(b_ref.at[0, i], b_ref.at[1, i], sfb.at[d], rfb.at[i], r, sib)
    for d in range(1, x_side):
        i = turn(x, d, x_side)
        copy(a_ref.at[0, i], a_ref.at[0, i], s3a.at[d], r3a.at[i], r, sib).wait_recv()
        go(a_ref.at[0, i], a_ref.at[1, i], sfa.at[d], rfa.at[i], r, sib)
    for i in range(side):
        copy(b_ref.at[0, i], b_ref.at[1, i], sfb.at[i], rfb.at[i], r, sib).wait_recv()
    for i in range(x_side):
        copy(a_ref.at[0, i], a_ref.at[1, i], sfa.at[i], rfa.at[i], r, sib).wait_recv()
    copy(eo_ref, eo_ref, se, re, r, sib).wait_recv()
    for one in sends:
        one.wait_send()


def gather_call(emb, fac, piv, sides=(X_SIDE, SIDE)):
    x_side, side = sides
    vmem = pl.BlockSpec(memory_space=pltpu.VMEM)
    anywhere = pl.BlockSpec(memory_space=pl.ANY)
    group = side * 2 * CAP
    cols, rank = emb.shape[1], fac.shape[1]
    dma = pltpu.SemaphoreType.DMA
    counts = [side, side, side, side, x_side, x_side, x_side, x_side, side, side, x_side, x_side, side, side]
    return pl.pallas_call(
        functools.partial(gather, sides),
        out_shape=(
            jax.ShapeDtypeStruct((2, x_side, side, group, cols), BF16),
            jax.ShapeDtypeStruct((2, side, x_side, group, rank), jnp.int16),
            jax.ShapeDtypeStruct((fac.shape[0], cols), BF16),
        ),
        in_specs=[anywhere, anywhere, vmem],
        out_specs=(vmem,) * 3,
        scratch_shapes=[
            pltpu.VMEM(emb.shape, BF16),
            pltpu.VMEM(fac.shape, F32),
            pltpu.VMEM((side, SUB, cols + rank), F32),
        ]
        + [dma((n,)) for n in counts]
        + [dma] * 4,
        compiler_params=pltpu.CompilerParams(
            collective_id=0, has_side_effects=True, vmem_limit_bytes=32 * 1024 * 1024
        ),
        name="gather_pivots",
    )(emb, fac, piv)


def pivot_places(piv, local_rows, sides):
    x_side, side = sides
    width = piv.shape[1]
    owner = ((piv.astype(F32) + 0.5) * (1.0 / local_rows)).astype(jnp.int32)
    lane = lax.broadcasted_iota(jnp.int32, piv.shape, 1)
    before = pltpu.roll(jnp.broadcast_to(owner, (SUB, width)), 1, axis=1)[0:1, :]
    again = jnp.where((before == owner) & (lane != 0) & (lane != width // 2), 1, 0)
    bits = side.bit_length() - 1
    return owner >> (2 * bits), (owner >> bits) & (side - 1), owner & (side - 1), again


def slot_rows(found, sides, core, part_x_first):
    x_side, side = sides
    x, z, y, again = found
    first = jnp.where(core == 0, z, y)
    other = jnp.where(core == 0, y, z)
    outer = x * side + other if part_x_first else other * x_side + x
    flat = ((outer * side + first) * CAP + again).astype(F32)
    return [
        jnp.transpose(jnp.broadcast_to(flat[:, at : at + TILE], (TILE, TILE)))
        for at in range(0, flat.shape[1], TILE)
    ]


def one_hot(tile, count):
    lane = lax.broadcasted_iota(jnp.int32, (TILE, TILE), 1).astype(F32)
    return jnp.concatenate(
        [jnp.where(tile == lane + float(at), 1.0, 0.0).astype(BF16) for at in range(0, count, TILE)], axis=1
    )


def extend(sides, piv_ref, a_ref, b_ref, emb_any, es, fo_any, res_ref, out_any, ro_ref, emb, fo, out_ref, pe, ps, pf, t_ref, q_ref, s_ref, cb_ref, pb_ref, sq_ref, le, lf, so):
    x_side, side = sides
    core = lax.axis_index("feat")
    width = pe.shape[0]
    own, cols = es.shape
    local_rows = emb_any.shape[0]
    rank = fo.shape[1]
    scale = 1.0 / (2 * cols)
    base = lax.axis_index("rows") * local_rows + core * own
    load_emb = pltpu.make_async_copy(emb_any.at[pl.ds(pl.multiple_of(core * own, own), own)], emb, le)
    load_fac = pltpu.make_async_copy(fo_any, fo, lf)
    load_emb.start()
    load_fac.start()
    pivots = jnp.concatenate([piv_ref[0:1, :], piv_ref[1:2, :]], axis=1)
    found = pivot_places(pivots, local_rows, sides)
    each = side * CAP
    slots = x_side * side * each
    per_block = width // 2 // TILE
    for block in range(2):
        rows = slice(block * each, (block + 1) * each)
        emb_own = a_ref[0, :, :, rows, :].reshape(slots, cols)
        emb_sib = a_ref[1, :, :, rows, :].reshape(slots, cols)
        fac_parts = []
        for at in range(2):
            ints = b_ref[at, :, :, rows, :].reshape(slots, rank).astype(jnp.int32).astype(F32)
            fac_parts.append(split2(ints))
        tiles = [
            slot_rows(found, sides, at_core, x_first)
            for x_first in (True, False)
            for at_core in (core, 1 - core)
        ]
        for t in range(block * per_block, (block + 1) * per_block):
            part = slice(t * TILE, (t + 1) * TILE)
            pe[part, :] = dot(one_hot(tiles[0][t], slots), emb_own, NN).astype(BF16)
            ps[part, :] = dot(one_hot(tiles[1][t], slots), emb_sib, NN).astype(BF16)
            ints = None
            for at in range(2):
                hot = one_hot(tiles[2 + at][t], slots)
                got = dot(hot, fac_parts[at][0], NN) + dot(hot, fac_parts[at][1], NN)
                ints = got if ints is None else ints + got
            pf[part, :] = ints * (FAC_MAX / LEVELS)

    def norms(one, two):
        one, two = one.astype(F32), two.astype(F32)
        return jnp.sum(one * one + two * two, axis=1, keepdims=True) * -0.5

    def fac_dot(left, right):
        return dot(jnp.concatenate([left[0], left[0], left[1]], axis=1), right, NT)

    high, low = split2(pf[...])
    right = jnp.concatenate([high, low, high], axis=1)
    pivot_lanes = norm_lanes(norms(pe[...], ps[...]), False)
    for start in range(0, width, TILE):
        part = slice(start, start + TILE)
        expo = dot(pe[part, :], pe[start:, :], NT) + dot(ps[part, :], ps[start:, :], NT)
        expo += dot(norm_lanes(norms(pe[part, :], ps[part, :]), True), pivot_lanes[start:, :], NT)
        row = lax.broadcasted_iota(jnp.int32, (TILE, width - start), 0)
        col = lax.broadcasted_iota(jnp.int32, (TILE, width - start), 1)
        value = jnp.exp(expo * scale) + jnp.where(row == col, ridge_weight, 0.0)
        t_ref[part, start:] = value - fac_dot(split2(pf[part, :]), right[start:, :])
    load_emb.wait()
    load_fac.wait()
    for start in range(0, own, TILE):
        part = slice(start, start + TILE)
        expo = dot(emb[part, :], pe[...], NT) + dot(es[part, :], ps[...], NT)
        expo += dot(norm_lanes(norms(emb[part, :], es[part, :]), True), pivot_lanes, NT)
        row = base + start + lax.broadcasted_iota(jnp.int32, (TILE, width), 0)
        value = jnp.exp(expo * scale) + jnp.where(row == pivots, ridge_weight, 0.0)
        q_ref[part, :] = value - fac_dot(split2(fo[part, :]), right)
    count = width // TILE
    tall = lax.broadcasted_iota(jnp.int32, (TILE, TILE), 0)
    flat = lax.broadcasted_iota(jnp.int32, (TILE, TILE), 1)

    def stack_left(pair, axis):
        return jnp.concatenate([pair[0], pair[0], pair[1]], axis=axis)

    def stack_right(pair, axis):
        return jnp.concatenate([pair[0], pair[1], pair[0]], axis=axis)

    def own_step(block, inverse, upper):
        here = slice(block * TILE, (block + 1) * TILE)
        fresh = dot(stack_left(split2(q_ref[:, here]), 1), stack_right(inverse, 1), NT)
        half, at = divmod(block * TILE, width // 2)
        out_ref[half, :, at : at + TILE] = fresh
        sq_ref[...] = fresh * fresh if block == 0 else sq_ref[...] + fresh * fresh
        if upper is not None:
            q_ref[:, (block + 1) * TILE :] -= dot(stack_left(split2(fresh), 1), stack_right(upper, 0), NN)

    late = None
    stores = [pltpu.make_async_copy(out_ref.at[i], out_any.at[i], so.at[i]) for i in range(2)]
    for block in range(count):
        here = slice(block * TILE, (block + 1) * TILE)
        s_ref[...] = t_ref[here, here]
        factor_tile(s_ref, cb_ref, pb_ref)
        if late is not None:
            own_step(*late)
        inverse = split2(jnp.where(flat <= tall, s_ref[...], 0.0))
        upper = None
        if block + 1 < count:
            rest = slice((block + 1) * TILE, width)
            upper = split2(dot(stack_left(inverse, 1), stack_right(split2(t_ref[here, rest]), 0), NN))
            for i in range(block + 1, count):
                rows = slice(i * TILE, (i + 1) * TILE)
                off = (i - block - 1) * TILE
                left = tuple(u[:, off : off + TILE] for u in upper)
                right = tuple(u[:, off:] for u in upper)
                t_ref[rows, i * TILE :] -= dot(stack_left(left, 0), stack_right(right, 0), TN)
        late = (block, inverse, upper)
        if block == count // 2:
            stores[0].start()
    own_step(*late)
    stores[1].start()
    hi, low = split2(sq_ref[...])
    ones = jnp.ones((SUB, TILE), BF16)
    removed = dot(ones, hi, NT) + dot(ones, low, NT)
    ro_ref[...] = res_ref[...] - removed[0:1, :].reshape(own)
    for one in stores:
        one.wait()


def extend_call(pivots, a, b, emb, es, fo, residual, sides=(X_SIDE, SIDE)):
    width = pivots.size
    own, rank = fo.shape
    cols = emb.shape[1]
    vmem = pl.BlockSpec(memory_space=pltpu.VMEM)
    anywhere = pl.BlockSpec(memory_space=pl.ANY)
    dma = pltpu.SemaphoreType.DMA
    return pl.pallas_call(
        functools.partial(extend, sides),
        out_shape=(
            jax.ShapeDtypeStruct((2, own, width // 2), F32),
            jax.ShapeDtypeStruct((own,), F32),
        ),
        in_specs=[vmem, vmem, vmem, anywhere, vmem, anywhere, vmem],
        out_specs=(anywhere, vmem),
        scratch_shapes=[
            pltpu.VMEM((own, cols), BF16),
            pltpu.VMEM((own, rank), F32),
            pltpu.VMEM((2, own, width // 2), F32),
            pltpu.VMEM((width, cols), BF16),
            pltpu.VMEM((width, cols), BF16),
            pltpu.VMEM((width, rank), F32),
            pltpu.VMEM((width, width), F32),
            pltpu.VMEM((own, width), F32),
            pltpu.VMEM((TILE, TILE), F32),
            pltpu.VMEM((SUB * SUB, TILE), F32),
            pltpu.VMEM((SUB * SUB, TILE), F32),
            pltpu.VMEM((own, TILE), F32),
            dma,
            dma,
            dma((2,)),
        ],
        compiler_params=pltpu.CompilerParams(vmem_limit_bytes=40 * 1024 * 1024),
        name="extend",
    )(pivots, a, b, emb, es, fo, residual)


def shards(sides, embeddings, factor, residual_diag, pivots):
    a, b, es = gather_call(embeddings, factor, pivots, sides)
    return extend_call(pivots, a, b, embeddings, es, factor, residual_diag, sides)


def solution(mesh):
    return jax.shard_map(
        functools.partial(shards, (X_SIDE, SIDE)),
        mesh=mesh,
        in_specs=(P("rows", "feat"), P(("rows", "feat"), None), P(("rows", "feat")), P()),
        out_specs=(P(None, ("rows", "feat"), None), P(("rows", "feat"))),
        check_vma=False,
    )
```

```python
import functools

import jax
import jax.numpy as jnp
from jax import lax
from jax.experimental import pallas as pl
from jax.experimental.pallas import tpu as pltpu
from jax.sharding import PartitionSpec as P

F32 = jnp.float32
BF16 = jnp.bfloat16
ridge_weight = 2.0
TILE = 128
CAP = 2
X_SIDE = 4
SIDE = 8
ROOM = 40 * 1024 * 1024
FAC_MAX = 0.1
LEVELS = 32767.0
MESH = pl.DeviceIdType.MESH
SUB = 8


def dot(a, b, dims):
    return lax.dot_general(a, b, (dims, ((), ())), preferred_element_type=F32)


NN = ((1,), (0,))
NT = ((1,), (1,))
TN = ((0,), (0,))


def split2(x):
    hi = x.astype(BF16)
    return hi, (x - hi.astype(F32)).astype(BF16)


def dot3(a, b, dims):
    return dot(a[0], b[0], dims) + (dot(a[0], b[1], dims) + dot(a[1], b[0], dims))


def norm_lanes(neg, first):
    hi = neg.astype(BF16).astype(F32)
    mid = (neg - hi).astype(BF16).astype(F32)
    low = (neg - hi) - mid
    lane = lax.broadcasted_iota(jnp.int32, (neg.shape[0], TILE), 1)
    at = 0 if first else 3
    out = jnp.where(lane < 6, 1.0, 0.0)
    out = jnp.where(lane == at, hi, out)
    out = jnp.where(lane == at + 1, mid, out)
    out = jnp.where(lane == at + 2, low, out)
    return out.astype(BF16)


def factor_tile(s_ref, cb_ref, pb_ref):
    count = TILE // SUB
    shape = (SUB, TILE)
    lane = lax.broadcasted_iota(jnp.int32, shape, 1)

    def rows(i):
        return s_ref[SUB * i : SUB * (i + 1), :]

    def lane_copy(x, at):
        return jnp.broadcast_to(x[:, at : at + 1], shape)

    def row_copy(ref, at):
        return jnp.broadcast_to(ref[at : at + 1, :], shape)

    ahead = [lane_copy(rows(0), j) for j in range(SUB)]
    for k in range(count):
        base = SUB * k
        diag = (lane >= base) & (lane < base + SUB)
        for j in range(SUB):
            cb_ref[SUB * j : SUB * (j + 1), :] = ahead[j]
        a = [[row_copy(cb_ref, SUB * q + m) if q <= m else None for q in range(SUB)] for m in range(SUB)]
        raw = {}
        for i in range(k + 1, count):
            block = rows(i)
            raw[i] = [lane_copy(block, base + j) for j in range(SUB)]
        near = {i: list(raw[i]) for i in range(k + 1, min(k + 3, count))}
        r = [jnp.where(diag, jnp.where(lane == base + j, 1.0, 0.0), row_copy(s_ref, base + j)) for j in range(SUB)]
        if k + 1 < count:
            block = rows(k + 1)
            ahead = [lane_copy(block, base + SUB + j) for j in range(SUB)]
        inv = []
        low = [[None] * SUB for _ in range(SUB)]
        for j in range(SUB):
            inv.append(lax.rsqrt(a[j][j]))
            for m in range(j + 1, SUB):
                low[m][j] = a[m][j] * inv[j]
            for q in range(j + 1, SUB):
                for m in range(q, SUB):
                    a[m][q] = a[m][q] - low[m][j] * low[q][j]
            for i in near:
                near[i][j] = near[i][j] * inv[j]
                for m in range(j + 1, SUB):
                    near[i][m] = near[i][m] - near[i][j] * low[m][j]
            if k + 1 < count:
                at = SUB * j
                pb_ref[at : at + SUB, :] = near[k + 1][j]
                for m in range(SUB):
                    ahead[m] = ahead[m] - near[k + 1][j] * row_copy(pb_ref, at + m)
            r[j] = r[j] * inv[j]
            for m in range(j + 1, SUB):
                r[m] = r[m] - low[m][j] * r[j]
        for j in range(SUB):
            s_ref[base + j : base + j + 1, :] = r[j][0:1, :]
        if k + 3 < count:
            z = list(r)
            for j in range(SUB - 1, -1, -1):
                z[j] = z[j] * inv[j]
                for m in range(j):
                    z[m] = z[m] - low[j][m] * z[j]
        for i in range(k + 1, count):
            left, right = (near[i], r) if i in near else (raw[i], z)
            total = jnp.where(diag, 0.0, rows(i))
            for j in range(SUB):
                total = total - left[j] * right[j]
            s_ref[SUB * i : SUB * (i + 1), :] = total


def places(sides):
    x_side, side = sides
    r = lax.axis_index("rows")
    core = lax.axis_index("feat")
    x = r // (side * side)
    z = lax.rem(r // side, side)
    y = lax.rem(r, side)
    first = z + core * (y - z)
    other = y + core * (z - y)
    first_step = side + core * (1 - side)
    other_step = 1 + core * (side - 1)
    return r, core, x, first, other, first_step, other_step


def gather(sides, emb_any, fac_any, piv_any, a_ref, b_ref, eo_ref, emb, fac, piv, g_ref, s1, r1, s2a, r2a, s2b, r2b, s3a, r3a, s3b, r3b, sfa, rfa, sfb, rfb, se, re, le, lf, lp):
    x_side, side = sides
    r, core, x, first, other, first_step, other_step = places(sides)
    sib = 1 - core
    cols = emb.shape[1]
    half = fac.shape[0]
    group = 2 * CAP

    load_emb = pltpu.make_async_copy(emb_any, emb, le)
    load_fac = pltpu.make_async_copy(fac_any, fac, lf)
    load_piv = pltpu.make_async_copy(piv_any, piv, lp)
    load_piv.start()
    load_emb.start()
    load_fac.start()

    def along_first(i):
        return r + (i - first) * first_step

    def along_other(i):
        return r + (i - other) * other_step

    def along_x(i):
        return r + (i - x) * (side * side)

    def turn(at, step, size):
        return lax.rem(at + step, size)

    barrier = pltpu.get_barrier_semaphore()

    def greet(row, at):
        pl.semaphore_signal(barrier, inc=1, device_id=(row, at), device_id_type=MESH)

    greet(r, sib)
    for d in range(1, side):
        greet(along_first(turn(first, d, side)), core)
        greet(along_other(turn(other, d, side)), core)
    for d in range(1, x_side):
        greet(along_x(turn(x, d, x_side)), core)

    start = r * emb.shape[0]
    load_piv.wait()
    ids = []
    for block in range(2):
        chosen = piv[block : block + 1, :]
        mine = (chosen >= start) & (chosen < start + emb.shape[0])
        least = jnp.min(jnp.where(mine, chosen, 1 << 30), axis=1, keepdims=True)
        most = jnp.max(jnp.where(mine, chosen, -1), axis=1, keepdims=True)
        ids += [least, jnp.where(most == least, -1, most)]

    def picks(count, offset):
        sub = lax.broadcasted_iota(jnp.int32, (2 * SUB, count), 0)
        row = lax.broadcasted_iota(jnp.int32, (2 * SUB, count), 1) + offset
        hot = jnp.zeros((2 * SUB, count), F32)
        for s, one in enumerate(ids):
            hot = jnp.where((sub == s) & (row == one), 1.0, hot)
        return hot.astype(BF16)

    hot_fac = picks(half, start + core * half)
    hot_emb = picks(emb.shape[0], start)
    load_emb.wait()
    g_ref[first, :, :cols] = dot(hot_emb, emb[...], NN)[:SUB]
    load_fac.wait()
    top, mid = split2(fac[...])
    own_fac = (dot(hot_fac, top, NN) + dot(hot_fac, mid, NN))[:SUB] * (LEVELS / FAC_MAX)
    own_fac = jnp.floor(own_fac + 0.5)
    g_ref[first, :, cols:] = jnp.clip(own_fac, -LEVELS, LEVELS)

    pl.semaphore_wait(barrier, 2 * (side - 1) + x_side)

    def copy(src, dst, send, recv, row, at):
        return pltpu.make_async_remote_copy(
            src_ref=src, dst_ref=dst, send_sem=send, recv_sem=recv, device_id=(row, at), device_id_type=MESH
        )

    sends = []

    def go(*args):
        one = copy(*args)
        one.start()
        sends.append(one)

    for d in range(1, side):
        to = along_first(turn(first, d, side))
        go(g_ref.at[first], g_ref.at[first], s1.at[d], r1.at[first], to, core)
    go(emb.at[pl.ds(pl.multiple_of(sib * half, half), half)], eo_ref, se, re, r, sib)
    to_row = lax.broadcasted_iota(jnp.int32, (group * side, SUB * side), 0)
    from_row = lax.broadcasted_iota(jnp.int32, (group * side, SUB * side), 1)
    half_rows = CAP * side
    block = jnp.where(to_row >= half_rows, 1, 0)
    inside = to_row - block * half_rows
    source = (inside >> 1) * SUB + block * CAP + (inside & 1)
    order = jnp.where(from_row == source, 1.0, 0.0).astype(BF16)
    for d in range(1, side):
        i = turn(first, d, side)
        copy(g_ref.at[i], g_ref.at[i], s1.at[d], r1.at[i], r, sib).wait_recv()
    held = g_ref[...].reshape(SUB * side, -1)
    a_ref[0, x, other] = dot(order, held[:, :cols].astype(BF16), NN).astype(BF16)
    for d in range(1, side):
        to = along_other(turn(other, d, side))
        go(a_ref.at[0, x, other], a_ref.at[0, x, other], s2a.at[d], r2a.at[other], to, core)
    top, mid = split2(held[:, cols:])
    ints = dot(order, top, NN) + dot(order, mid, NN)
    b_ref[0, other, x] = ints.astype(jnp.int32).astype(jnp.int16)
    for d in range(1, x_side):
        to = along_x(turn(x, d, x_side))
        go(b_ref.at[0, other, x], b_ref.at[0, other, x], s2b.at[d], r2b.at[x], to, core)

    def spread_a(i, slot):
        for d in range(1, x_side):
            to = along_x(turn(x, d, x_side))
            go(a_ref.at[0, x, i], a_ref.at[0, x, i], s3a.at[slot, d], r3a.at[x, i], to, core)

    def spread_b(i, slot):
        for d in range(1, side):
            to = along_other(turn(other, d, side))
            go(b_ref.at[0, other, i], b_ref.at[0, other, i], s3b.at[slot, d], r3b.at[other, i], to, core)

    spread_a(other, 0)
    spread_b(x, 0)
    b_turns = [1, x_side - 1] + list(range(2, x_side - 1))
    a_turns = [d for pair in zip(range(1, side // 2), range(side - 1, side // 2, -1)) for d in pair] + [side // 2]
    for n, d in enumerate(a_turns):
        i = turn(other, d, side)
        copy(a_ref.at[0, x, i], a_ref.at[0, x, i], s2a.at[d], r2a.at[i], r, sib).wait_recv()
        spread_a(i, d)
        if n % 2 == 1 and n // 2 < len(b_turns):
            d = b_turns[n // 2]
            i = turn(x, d, x_side)
            copy(b_ref.at[0, other, i], b_ref.at[0, other, i], s2b.at[d], r2b.at[i], r, sib).wait_recv()
            spread_b(i, d)

    go(a_ref.at[0, x], a_ref.at[1, x], sfa.at[0], rfa.at[x], r, sib)
    go(b_ref.at[0, other], b_ref.at[1, other], sfb.at[0], rfb.at[other], r, sib)

    def pass_a(d):
        i = turn(x, d, x_side)
        for j in range(side):
            copy(a_ref.at[0, i, j], a_ref.at[0, i, j], s3a.at[0, d], r3a.at[i, j], r, sib).wait_recv()
        go(a_ref.at[0, i], a_ref.at[1, i], sfa.at[d], rfa.at[i], r, sib)

    def pass_b(d):
        i = turn(other, d, side)
        for j in range(x_side):
            copy(b_ref.at[0, i, j], b_ref.at[0, i, j], s3b.at[0, d], r3b.at[i, j], r, sib).wait_recv()
        go(b_ref.at[0, i], b_ref.at[1, i], sfb.at[d], rfb.at[i], r, sib)

    for d in a_turns[:4]:
        pass_b(d)
    for d in b_turns:
        pass_a(d)
    for d in a_turns[4:]:
        pass_b(d)
    for i in range(side):
        copy(b_ref.at[0, i], b_ref.at[1, i], sfb.at[i], rfb.at[i], r, sib).wait_recv()
    for i in range(x_side):
        copy(a_ref.at[0, i], a_ref.at[1, i], sfa.at[i], rfa.at[i], r, sib).wait_recv()
    copy(eo_ref, eo_ref, se, re, r, sib).wait_recv()
    for one in sends:
        one.wait_send()


def gather_call(emb, fac, piv, sides=(X_SIDE, SIDE)):
    x_side, side = sides
    vmem = pl.BlockSpec(memory_space=pltpu.VMEM)
    far = pl.BlockSpec(memory_space=pltpu.HBM)
    group = side * 2 * CAP
    cols, rank = emb.shape[1], fac.shape[1]
    dma = pltpu.SemaphoreType.DMA
    counts = [side, side, side, side, x_side, x_side, (side, x_side), (x_side, side), (x_side, side), (side, x_side), x_side, x_side, side, side]
    return pl.pallas_call(
        functools.partial(gather, sides),
        out_shape=(
            jax.ShapeDtypeStruct((2, x_side, side, group, cols), BF16),
            jax.ShapeDtypeStruct((2, side, x_side, group, rank), jnp.int16),
            jax.ShapeDtypeStruct((fac.shape[0], cols), BF16),
        ),
        in_specs=[far] * 3,
        out_specs=(vmem,) * 3,
        scratch_shapes=[
            pltpu.VMEM(emb.shape, BF16),
            pltpu.VMEM(fac.shape, F32),
            pltpu.VMEM(piv.shape, jnp.int32),
            pltpu.VMEM((side, SUB, cols + rank), F32),
        ]
        + [dma(n if isinstance(n, tuple) else (n,)) for n in counts]
        + [dma] * 5,
        compiler_params=pltpu.CompilerParams(
            collective_id=0, has_side_effects=True, vmem_limit_bytes=ROOM
        ),
        name="gather_pivots",
    )(emb, fac, piv)


def pivot_places(piv, local_rows, sides):
    x_side, side = sides
    width = piv.shape[1]
    owner = ((piv.astype(F32) + 0.5) * (1.0 / local_rows)).astype(jnp.int32)
    lane = lax.broadcasted_iota(jnp.int32, piv.shape, 1)
    before = pltpu.roll(jnp.broadcast_to(owner, (SUB, width)), 1, axis=1)[0:1, :]
    again = jnp.where((before == owner) & (lane != 0) & (lane != width // 2), 1, 0)
    bits = side.bit_length() - 1
    return owner >> (2 * bits), (owner >> bits) & (side - 1), owner & (side - 1), again


def slot_rows(found, sides, core, part_x_first):
    x_side, side = sides
    x, z, y, again = found
    first = jnp.where(core == 0, z, y)
    other = jnp.where(core == 0, y, z)
    outer = x * side + other if part_x_first else other * x_side + x
    flat = ((outer * side + first) * CAP + again).astype(F32)
    return [
        jnp.transpose(jnp.broadcast_to(flat[:, at : at + TILE], (TILE, TILE)))
        for at in range(0, flat.shape[1], TILE)
    ]


def one_hot(tile, count):
    lane = lax.broadcasted_iota(jnp.int32, (TILE, TILE), 1).astype(F32)
    return jnp.concatenate(
        [jnp.where(tile == lane + float(at), 1.0, 0.0).astype(BF16) for at in range(0, count, TILE)], axis=1
    )


def extend(sides, piv_any, a_ref, b_ref, emb_any, es, fo_any, res_any, out_any, ro_any, piv_ref, res_ref, ro_ref, emb, fo, out_ref, pe, ps, pf, t_ref, q_ref, s_ref, cb_ref, pb_ref, sq_ref, le, lf, lp, lr, so):
    x_side, side = sides
    core = lax.axis_index("feat")
    width = pe.shape[0]
    own, cols = es.shape
    local_rows = emb_any.shape[0]
    rank = fo.shape[1]
    scale = 1.0 / (2 * cols)
    base = lax.axis_index("rows") * local_rows + core * own
    load_emb = pltpu.make_async_copy(emb_any.at[pl.ds(pl.multiple_of(core * own, own), own)], emb, le)
    load_fac = pltpu.make_async_copy(fo_any, fo, lf)
    load_emb.start()
    load_fac.start()
    load_piv = pltpu.make_async_copy(piv_any, piv_ref, lp)
    load_res = pltpu.make_async_copy(res_any, res_ref, lr)
    load_piv.start()
    load_res.start()
    load_piv.wait()
    pivots = jnp.concatenate([piv_ref[0:1, :], piv_ref[1:2, :]], axis=1)
    found = pivot_places(pivots, local_rows, sides)
    each = side * CAP
    slots = x_side * side * each
    per_block = width // 2 // TILE
    for block in range(2):
        rows = slice(block * each, (block + 1) * each)
        emb_own = a_ref[0, :, :, rows, :].reshape(slots, cols)
        emb_sib = a_ref[1, :, :, rows, :].reshape(slots, cols)
        fac_parts = []
        for at in range(2):
            ints = b_ref[at, :, :, rows, :].reshape(slots, rank).astype(jnp.int32).astype(F32)
            fac_parts.append(split2(ints))
        tiles = [
            slot_rows(found, sides, at_core, x_first)
            for x_first in (True, False)
            for at_core in (core, 1 - core)
        ]
        for t in range(block * per_block, (block + 1) * per_block):
            part = slice(t * TILE, (t + 1) * TILE)
            pe[part, :] = dot(one_hot(tiles[0][t], slots), emb_own, NN).astype(BF16)
            ps[part, :] = dot(one_hot(tiles[1][t], slots), emb_sib, NN).astype(BF16)
            ints = None
            for at in range(2):
                hot = one_hot(tiles[2 + at][t], slots)
                got = dot(hot, fac_parts[at][0], NN) + dot(hot, fac_parts[at][1], NN)
                ints = got if ints is None else ints + got
            pf[part, :] = ints * (FAC_MAX / LEVELS)

    def norms(one, two):
        one, two = one.astype(F32), two.astype(F32)
        return jnp.sum(one * one + two * two, axis=1, keepdims=True) * -0.5

    def fac_dot(left, right):
        return dot(jnp.concatenate([left[0], left[0], left[1]], axis=1), right, NT)

    high, low = split2(pf[...])
    right = jnp.concatenate([high, low, high], axis=1)
    pivot_lanes = norm_lanes(norms(pe[...], ps[...]), False)
    for start in range(0, width, TILE):
        part = slice(start, start + TILE)
        expo = dot(pe[part, :], pe[start:, :], NT) + dot(ps[part, :], ps[start:, :], NT)
        expo += dot(norm_lanes(norms(pe[part, :], ps[part, :]), True), pivot_lanes[start:, :], NT)
        row = lax.broadcasted_iota(jnp.int32, (TILE, width - start), 0)
        col = lax.broadcasted_iota(jnp.int32, (TILE, width - start), 1)
        value = jnp.exp(expo * scale) + jnp.where(row == col, ridge_weight, 0.0)
        t_ref[part, start:] = value - fac_dot(split2(pf[part, :]), right[start:, :])
    load_emb.wait()
    load_fac.wait()
    for start in range(0, own, TILE):
        part = slice(start, start + TILE)
        expo = dot(emb[part, :], pe[...], NT) + dot(es[part, :], ps[...], NT)
        expo += dot(norm_lanes(norms(emb[part, :], es[part, :]), True), pivot_lanes, NT)
        row = base + start + lax.broadcasted_iota(jnp.int32, (TILE, width), 0)
        value = jnp.exp(expo * scale) + jnp.where(row == pivots, ridge_weight, 0.0)
        q_ref[part, :] = value - fac_dot(split2(fo[part, :]), right)
    count = width // TILE
    tall = lax.broadcasted_iota(jnp.int32, (TILE, TILE), 0)
    flat = lax.broadcasted_iota(jnp.int32, (TILE, TILE), 1)

    def stack_left(pair, axis):
        return jnp.concatenate([pair[0], pair[0], pair[1]], axis=axis)

    def stack_right(pair, axis):
        return jnp.concatenate([pair[0], pair[1], pair[0]], axis=axis)

    def own_step(block, inverse, upper):
        here = slice(block * TILE, (block + 1) * TILE)
        fresh = dot(stack_left(split2(q_ref[:, here]), 1), stack_right(inverse, 1), NT)
        half, at = divmod(block * TILE, width // 2)
        out_ref[half, :, at : at + TILE] = fresh
        sq_ref[...] = fresh * fresh if block == 0 else sq_ref[...] + fresh * fresh
        if upper is not None:
            q_ref[:, (block + 1) * TILE :] -= dot(stack_left(split2(fresh), 1), stack_right(upper, 0), NN)

    late = None
    stores = [pltpu.make_async_copy(out_ref.at[i], out_any.at[i], so.at[i]) for i in range(2)]
    for block in range(count):
        here = slice(block * TILE, (block + 1) * TILE)
        s_ref[...] = t_ref[here, here]
        factor_tile(s_ref, cb_ref, pb_ref)
        if late is not None:
            own_step(*late)
        inverse = split2(jnp.where(flat <= tall, s_ref[...], 0.0))
        upper = None
        if block + 1 < count:
            rest = slice((block + 1) * TILE, width)
            upper = split2(dot(stack_left(inverse, 1), stack_right(split2(t_ref[here, rest]), 0), NN))
            for i in range(block + 1, count):
                rows = slice(i * TILE, (i + 1) * TILE)
                off = (i - block - 1) * TILE
                left = tuple(u[:, off : off + TILE] for u in upper)
                right = tuple(u[:, off:] for u in upper)
                t_ref[rows, i * TILE :] -= dot(stack_left(left, 0), stack_right(right, 0), TN)
        late = (block, inverse, upper)
        if block == count // 2:
            stores[0].start()
    own_step(*late)
    stores[1].start()
    hi, low = split2(sq_ref[...])
    ones = jnp.ones((SUB, TILE), BF16)
    removed = dot(ones, hi, NT) + dot(ones, low, NT)
    load_res.wait()
    ro_ref[...] = res_ref[...] - removed[0:1, :].reshape(own)
    stores.append(pltpu.make_async_copy(ro_ref, ro_any, so.at[2]))
    stores[2].start()
    for one in stores:
        one.wait()


def extend_call(pivots, a, b, emb, es, fo, residual, sides=(X_SIDE, SIDE)):
    width = pivots.size
    own, rank = fo.shape
    cols = emb.shape[1]
    vmem = pl.BlockSpec(memory_space=pltpu.VMEM)
    far = pl.BlockSpec(memory_space=pltpu.HBM)
    dma = pltpu.SemaphoreType.DMA
    return pl.pallas_call(
        functools.partial(extend, sides),
        out_shape=(
            jax.ShapeDtypeStruct((2, own, width // 2), F32),
            jax.ShapeDtypeStruct((own,), F32),
        ),
        in_specs=[far, vmem, vmem, far, vmem, far, far],
        out_specs=(far, far),
        scratch_shapes=[
            pltpu.VMEM(pivots.shape, jnp.int32),
            pltpu.VMEM((own,), F32),
            pltpu.VMEM((own,), F32),
            pltpu.VMEM((own, cols), BF16),
            pltpu.VMEM((own, rank), F32),
            pltpu.VMEM((2, own, width // 2), F32),
            pltpu.VMEM((width, cols), BF16),
            pltpu.VMEM((width, cols), BF16),
            pltpu.VMEM((width, rank), F32),
            pltpu.VMEM((width, width), F32),
            pltpu.VMEM((own, width), F32),
            pltpu.VMEM((TILE, TILE), F32),
            pltpu.VMEM((SUB * SUB, TILE), F32),
            pltpu.VMEM((SUB * SUB, TILE), F32),
            pltpu.VMEM((own, TILE), F32),
            dma,
            dma,
            dma,
            dma,
            dma((3,)),
        ],
        compiler_params=pltpu.CompilerParams(vmem_limit_bytes=ROOM),
        name="extend",
    )(pivots, a, b, emb, es, fo, residual)


def shards(sides, *given):
    embeddings, factor, residual_diag, pivots = (pltpu.with_memory_space_constraint(one, pltpu.HBM) for one in given)
    a, b, es = gather_call(embeddings, factor, pivots, sides)
    return extend_call(pivots, a, b, embeddings, es, factor, residual_diag, sides)


def solution(mesh):
    return jax.shard_map(
        functools.partial(shards, (X_SIDE, SIDE)),
        mesh=mesh,
        in_specs=(P("rows", "feat"), P(("rows", "feat"), None), P(("rows", "feat")), P()),
        out_specs=(P(None, ("rows", "feat"), None), P(("rows", "feat"))),
        check_vma=False,
    )
```

```python
import functools

import jax
import jax.numpy as jnp
from jax import lax
from jax.experimental import pallas as pl
from jax.experimental.pallas import tpu as pltpu
from jax.sharding import PartitionSpec as P

F32 = jnp.float32
BF16 = jnp.bfloat16
ridge_weight = 2.0
TILE = 128
CAP = 2
GROUPS = 4
X_SIDE = 4
SIDE = 8
ROOM = 40 * 1024 * 1024
FAC_MAX = 0.1
LEVELS = 32767.0
MESH = pl.DeviceIdType.MESH
SUB = 8


def dot(a, b, dims):
    return lax.dot_general(a, b, (dims, ((), ())), preferred_element_type=F32)


NN = ((1,), (0,))
NT = ((1,), (1,))
TN = ((0,), (0,))


def split2(x):
    hi = x.astype(BF16)
    return hi, (x - hi.astype(F32)).astype(BF16)


def dot3(a, b, dims):
    return dot(a[0], b[0], dims) + (dot(a[0], b[1], dims) + dot(a[1], b[0], dims))


def norm_lanes(neg, first):
    hi = neg.astype(BF16).astype(F32)
    mid = (neg - hi).astype(BF16).astype(F32)
    low = (neg - hi) - mid
    lane = lax.broadcasted_iota(jnp.int32, (neg.shape[0], TILE), 1)
    at = 0 if first else 3
    out = jnp.where(lane < 6, 1.0, 0.0)
    out = jnp.where(lane == at, hi, out)
    out = jnp.where(lane == at + 1, mid, out)
    out = jnp.where(lane == at + 2, low, out)
    return out.astype(BF16)


def factor_tile(s_ref, cb_ref, pb_ref):
    count = TILE // SUB
    shape = (SUB, TILE)
    lane = lax.broadcasted_iota(jnp.int32, shape, 1)

    def rows(i):
        return s_ref[SUB * i : SUB * (i + 1), :]

    def lane_copy(x, at):
        return jnp.broadcast_to(x[:, at : at + 1], shape)

    def row_copy(ref, at):
        return jnp.broadcast_to(ref[at : at + 1, :], shape)

    ahead = [lane_copy(rows(0), j) for j in range(SUB)]
    for k in range(count):
        base = SUB * k
        diag = (lane >= base) & (lane < base + SUB)
        for j in range(SUB):
            cb_ref[SUB * j : SUB * (j + 1), :] = ahead[j]
        a = [[row_copy(cb_ref, SUB * q + m) if q <= m else None for q in range(SUB)] for m in range(SUB)]
        raw = {}
        for i in range(k + 1, count):
            block = rows(i)
            raw[i] = [lane_copy(block, base + j) for j in range(SUB)]
        near = {i: list(raw[i]) for i in range(k + 1, min(k + 3, count))}
        r = [jnp.where(diag, jnp.where(lane == base + j, 1.0, 0.0), row_copy(s_ref, base + j)) for j in range(SUB)]
        if k + 1 < count:
            block = rows(k + 1)
            ahead = [lane_copy(block, base + SUB + j) for j in range(SUB)]
        inv = []
        low = [[None] * SUB for _ in range(SUB)]
        for j in range(SUB):
            inv.append(lax.rsqrt(a[j][j]))
            for m in range(j + 1, SUB):
                low[m][j] = a[m][j] * inv[j]
            for q in range(j + 1, SUB):
                for m in range(q, SUB):
                    a[m][q] = a[m][q] - low[m][j] * low[q][j]
            for i in near:
                near[i][j] = near[i][j] * inv[j]
                for m in range(j + 1, SUB):
                    near[i][m] = near[i][m] - near[i][j] * low[m][j]
            if k + 1 < count:
                at = SUB * j
                pb_ref[at : at + SUB, :] = near[k + 1][j]
                for m in range(SUB):
                    ahead[m] = ahead[m] - near[k + 1][j] * row_copy(pb_ref, at + m)
            r[j] = r[j] * inv[j]
            for m in range(j + 1, SUB):
                r[m] = r[m] - low[m][j] * r[j]
        for j in range(SUB):
            s_ref[base + j : base + j + 1, :] = r[j][0:1, :]
        if k + 3 < count:
            z = list(r)
            for j in range(SUB - 1, -1, -1):
                z[j] = z[j] * inv[j]
                for m in range(j):
                    z[m] = z[m] - low[j][m] * z[j]
        for i in range(k + 1, count):
            left, right = (near[i], r) if i in near else (raw[i], z)
            total = jnp.where(diag, 0.0, rows(i))
            for j in range(SUB):
                total = total - left[j] * right[j]
            s_ref[SUB * i : SUB * (i + 1), :] = total


def places(sides):
    x_side, side = sides
    r = lax.axis_index("rows")
    core = lax.axis_index("feat")
    x = r // (side * side)
    z = lax.rem(r // side, side)
    y = lax.rem(r, side)
    first = z + core * (y - z)
    other = y + core * (z - y)
    first_step = side + core * (1 - side)
    other_step = 1 + core * (side - 1)
    return r, core, x, first, other, first_step, other_step


def gather(sides, emb_any, fac_any, piv_any, a_ref, b_ref, eo_ref, emb, fac, piv, g_ref, s1, r1, s2a, r2a, s2b, r2b, s3a, r3a, s3b, r3b, sfa, rfa, sfb, rfb, se, re, le, lf, lp):
    x_side, side = sides
    r, core, x, first, other, first_step, other_step = places(sides)
    sib = 1 - core
    cols = emb.shape[1]
    half = fac.shape[0]
    group = 2 * CAP

    load_emb = pltpu.make_async_copy(emb_any, emb, le)
    load_fac = pltpu.make_async_copy(fac_any, fac, lf)
    load_piv = pltpu.make_async_copy(piv_any, piv, lp)
    load_piv.start()
    load_emb.start()
    load_fac.start()

    def along_first(i):
        return r + (i - first) * first_step

    def along_other(i):
        return r + (i - other) * other_step

    def along_x(i):
        return r + (i - x) * (side * side)

    def turn(at, step, size):
        return lax.rem(at + step, size)

    barrier = pltpu.get_barrier_semaphore()

    def greet(row, at):
        pl.semaphore_signal(barrier, inc=1, device_id=(row, at), device_id_type=MESH)

    greet(r, sib)
    for d in range(1, side):
        greet(along_first(turn(first, d, side)), core)
        greet(along_other(turn(other, d, side)), core)
    for d in range(1, x_side):
        greet(along_x(turn(x, d, x_side)), core)

    start = r * emb.shape[0]
    load_piv.wait()
    ids = []
    for block in range(2):
        chosen = piv[block : block + 1, :]
        mine = (chosen >= start) & (chosen < start + emb.shape[0])
        least = jnp.min(jnp.where(mine, chosen, 1 << 30), axis=1, keepdims=True)
        most = jnp.max(jnp.where(mine, chosen, -1), axis=1, keepdims=True)
        ids += [least, jnp.where(most == least, -1, most)]

    def picks(count, offset):
        sub = lax.broadcasted_iota(jnp.int32, (GROUPS * group, count), 0) & (group - 1)
        row = lax.broadcasted_iota(jnp.int32, (GROUPS * group, count), 1) + offset
        hot = jnp.zeros((GROUPS * group, count), F32)
        for s, one in enumerate(ids):
            hot = jnp.where((sub == s) & (row == one), 1.0, hot)
        return hot.astype(BF16)

    hot_fac = picks(half, start + core * half)
    hot_emb = picks(emb.shape[0], start)
    load_fac.wait()
    top, mid = split2(fac[...])
    ints = (dot(hot_fac, top, NN) + dot(hot_fac, mid, NN)) * (LEVELS / FAC_MAX)
    ints = jnp.clip(jnp.floor(ints + 0.5), -LEVELS, LEVELS)
    high = ints.astype(BF16).astype(F32)
    low = ints - high
    load_emb.wait()
    taken = dot(hot_emb, emb[...], NN)
    part = lax.broadcasted_iota(jnp.int32, (GROUPS * group, TILE), 0) // group
    sources = [taken[:, :TILE], taken[:, 2 * TILE :], high[:, TILE:], low[:, TILE:]]
    left = sources[0]
    for n in range(1, GROUPS):
        left = jnp.where(part == n, sources[n], left)
    right = jnp.where(part == 0, taken[:, TILE : 2 * TILE], 0.0)
    right = jnp.where(part == 1, high[:, :TILE], right)
    right = jnp.where(part == 2, low[:, :TILE], right)
    g_ref[first, :, :TILE] = left.astype(BF16)
    g_ref[first, :, TILE:] = right.astype(BF16)

    pl.semaphore_wait(barrier, 2 * (side - 1) + x_side)

    def copy(src, dst, send, recv, row, at):
        return pltpu.make_async_remote_copy(
            src_ref=src, dst_ref=dst, send_sem=send, recv_sem=recv, device_id=(row, at), device_id_type=MESH
        )

    sends = []

    def go(*args):
        one = copy(*args)
        one.start()
        sends.append(one)

    for d in range(1, side):
        to = along_first(turn(first, d, side))
        go(g_ref.at[first], g_ref.at[first], s1.at[d], r1.at[first], to, core)
    to_row = lax.broadcasted_iota(jnp.int32, (group * side, GROUPS * group * side), 0)
    from_row = lax.broadcasted_iota(jnp.int32, (group * side, GROUPS * group * side), 1)
    half_rows = CAP * side
    block = jnp.where(to_row >= half_rows, 1, 0)
    inside = to_row - block * half_rows
    source = (inside >> 1) * (GROUPS * group) + block * CAP + (inside & 1)
    orders = [jnp.where(from_row == source + n * group, 1.0, 0.0).astype(BF16) for n in range(GROUPS)]
    for d in range(1, side):
        i = turn(first, d, side)
        copy(g_ref.at[i], g_ref.at[i], s1.at[d], r1.at[i], r, sib).wait_recv()
    held = g_ref[...].reshape(GROUPS * group * side, 2 * TILE)
    outs = [dot(order, held, NN) for order in orders]
    a_ref[0, x, other, :, : 2 * TILE] = outs[0].astype(BF16)
    a_ref[0, x, other, :, 2 * TILE :] = outs[1][:, :TILE].astype(BF16)
    for d in range(1, side):
        to = along_other(turn(other, d, side))
        go(a_ref.at[0, x, other], a_ref.at[0, x, other], s2a.at[d], r2a.at[other], to, core)
    ints = (outs[1][:, TILE:] + outs[2][:, TILE:], outs[2][:, :TILE] + outs[3][:, :TILE])
    for n in range(2):
        b_ref[0, other, x, :, n * TILE : (n + 1) * TILE] = ints[n].astype(jnp.int32).astype(jnp.int16)
    for d in range(1, x_side):
        to = along_x(turn(x, d, x_side))
        go(b_ref.at[0, other, x], b_ref.at[0, other, x], s2b.at[d], r2b.at[x], to, core)

    def spread_a(i, slot):
        for d in range(1, x_side):
            to = along_x(turn(x, d, x_side))
            go(a_ref.at[0, x, i], a_ref.at[0, x, i], s3a.at[slot, d], r3a.at[x, i], to, core)

    def spread_b(i, slot):
        for d in range(1, side):
            to = along_other(turn(other, d, side))
            go(b_ref.at[0, other, i], b_ref.at[0, other, i], s3b.at[slot, d], r3b.at[other, i], to, core)

    spread_a(other, 0)
    spread_b(x, 0)
    go(emb.at[pl.ds(pl.multiple_of(sib * half, half), half)], eo_ref, se, re, r, sib)
    b_turns = [1, x_side - 1] + list(range(2, x_side - 1))
    a_turns = [d for pair in zip(range(1, side // 2), range(side - 1, side // 2, -1)) for d in pair] + [side // 2]
    for n, d in enumerate(a_turns):
        i = turn(other, d, side)
        copy(a_ref.at[0, x, i], a_ref.at[0, x, i], s2a.at[d], r2a.at[i], r, sib).wait_recv()
        spread_a(i, d)
        if n % 2 == 1 and n // 2 < len(b_turns):
            d = b_turns[n // 2]
            i = turn(x, d, x_side)
            copy(b_ref.at[0, other, i], b_ref.at[0, other, i], s2b.at[d], r2b.at[i], r, sib).wait_recv()
            spread_b(i, d)

    go(a_ref.at[0, x], a_ref.at[1, x], sfa.at[0, 0], rfa.at[x, 0], r, sib)
    go(b_ref.at[0, other], b_ref.at[1, other], sfb.at[0], rfb.at[other], r, sib)

    def pass_a(d, j):
        i = turn(x, d, x_side)
        copy(a_ref.at[0, i, j], a_ref.at[0, i, j], s3a.at[0, d], r3a.at[i, j], r, sib).wait_recv()
        go(a_ref.at[0, i, j], a_ref.at[1, i, j], sfa.at[d, j], rfa.at[i, j], r, sib)

    def pass_b(d):
        i = turn(other, d, side)
        for j in range(x_side):
            copy(b_ref.at[0, i, j], b_ref.at[0, i, j], s3b.at[0, d], r3b.at[i, j], r, sib).wait_recv()
        go(b_ref.at[0, i], b_ref.at[1, i], sfb.at[d], rfb.at[i], r, sib)

    for n, e in enumerate([0] + a_turns):
        j = turn(other, e, side)
        for d in b_turns:
            pass_a(d, j)
        if n >= side - 4:
            pass_b(a_turns[n - side + 4])
    for d in a_turns[4:]:
        pass_b(d)
    for i in range(side):
        copy(b_ref.at[0, i], b_ref.at[1, i], sfb.at[i], rfb.at[i], r, sib).wait_recv()
    copy(a_ref.at[0, x], a_ref.at[1, x], sfa.at[0, 0], rfa.at[x, 0], r, sib).wait_recv()
    for d in range(1, x_side):
        i = turn(x, d, x_side)
        for j in range(side):
            copy(a_ref.at[0, i, j], a_ref.at[1, i, j], sfa.at[d, j], rfa.at[i, j], r, sib).wait_recv()
    copy(eo_ref, eo_ref, se, re, r, sib).wait_recv()
    for one in sends:
        one.wait_send()


def gather_call(emb, fac, piv, sides=(X_SIDE, SIDE)):
    x_side, side = sides
    vmem = pl.BlockSpec(memory_space=pltpu.VMEM)
    far = pl.BlockSpec(memory_space=pltpu.HBM)
    group = side * 2 * CAP
    cols, rank = emb.shape[1], fac.shape[1]
    dma = pltpu.SemaphoreType.DMA
    counts = [side, side, side, side, x_side, x_side, (side, x_side), (x_side, side), (x_side, side), (side, x_side), (x_side, side), (x_side, side), side, side]
    return pl.pallas_call(
        functools.partial(gather, sides),
        out_shape=(
            jax.ShapeDtypeStruct((2, x_side, side, group, cols), BF16),
            jax.ShapeDtypeStruct((2, side, x_side, group, rank), jnp.int16),
            jax.ShapeDtypeStruct((fac.shape[0], cols), BF16),
        ),
        in_specs=[far] * 3,
        out_specs=(vmem,) * 3,
        scratch_shapes=[
            pltpu.VMEM(emb.shape, BF16),
            pltpu.VMEM(fac.shape, F32),
            pltpu.VMEM(piv.shape, jnp.int32),
            pltpu.VMEM((side, GROUPS * group // side, 2 * TILE), BF16),
        ]
        + [dma(n if isinstance(n, tuple) else (n,)) for n in counts]
        + [dma] * 5,
        compiler_params=pltpu.CompilerParams(
            collective_id=0, has_side_effects=True, vmem_limit_bytes=ROOM
        ),
        name="gather_pivots",
    )(emb, fac, piv)


def pivot_places(piv, local_rows, sides):
    x_side, side = sides
    width = piv.shape[1]
    owner = ((piv.astype(F32) + 0.5) * (1.0 / local_rows)).astype(jnp.int32)
    lane = lax.broadcasted_iota(jnp.int32, piv.shape, 1)
    before = pltpu.roll(jnp.broadcast_to(owner, (SUB, width)), 1, axis=1)[0:1, :]
    again = jnp.where((before == owner) & (lane != 0) & (lane != width // 2), 1, 0)
    bits = side.bit_length() - 1
    return owner >> (2 * bits), (owner >> bits) & (side - 1), owner & (side - 1), again


def slot_rows(found, sides, core, part_x_first):
    x_side, side = sides
    x, z, y, again = found
    first = jnp.where(core == 0, z, y)
    other = jnp.where(core == 0, y, z)
    outer = x * side + other if part_x_first else other * x_side + x
    flat = ((outer * side + first) * CAP + again).astype(F32)
    return [
        jnp.transpose(jnp.broadcast_to(flat[:, at : at + TILE], (TILE, TILE)))
        for at in range(0, flat.shape[1], TILE)
    ]


def one_hot(tile, count):
    lane = lax.broadcasted_iota(jnp.int32, (TILE, TILE), 1).astype(F32)
    return jnp.concatenate(
        [jnp.where(tile == lane + float(at), 1.0, 0.0).astype(BF16) for at in range(0, count, TILE)], axis=1
    )


def extend(sides, piv_any, a_ref, b_ref, emb_any, es, fo_any, res_any, out_any, ro_any, piv_ref, res_ref, ro_ref, emb, fo, out_ref, pe, ps, pf, t_ref, q_ref, s_ref, cb_ref, pb_ref, sq_ref, le, lf, lp, lr, so):
    x_side, side = sides
    core = lax.axis_index("feat")
    width = pe.shape[0]
    own, cols = es.shape
    local_rows = emb_any.shape[0]
    rank = fo.shape[1]
    scale = 1.0 / (2 * cols)
    base = lax.axis_index("rows") * local_rows + core * own
    load_emb = pltpu.make_async_copy(emb_any.at[pl.ds(pl.multiple_of(core * own, own), own)], emb, le)
    load_fac = pltpu.make_async_copy(fo_any, fo, lf)
    load_emb.start()
    load_fac.start()
    load_piv = pltpu.make_async_copy(piv_any, piv_ref, lp)
    load_res = pltpu.make_async_copy(res_any, res_ref, lr)
    load_piv.start()
    load_res.start()
    load_piv.wait()
    pivots = jnp.concatenate([piv_ref[0:1, :], piv_ref[1:2, :]], axis=1)
    found = pivot_places(pivots, local_rows, sides)
    each = side * CAP
    slots = x_side * side * each
    per_block = width // 2 // TILE
    for block in range(2):
        rows = slice(block * each, (block + 1) * each)
        emb_own = a_ref[0, :, :, rows, :].reshape(slots, cols)
        emb_sib = a_ref[1, :, :, rows, :].reshape(slots, cols)
        fac_parts = []
        for at in range(2):
            ints = b_ref[at, :, :, rows, :].reshape(slots, rank).astype(jnp.int32).astype(F32)
            fac_parts.append(split2(ints))
        tiles = [
            slot_rows(found, sides, at_core, x_first)
            for x_first in (True, False)
            for at_core in (core, 1 - core)
        ]
        for t in range(block * per_block, (block + 1) * per_block):
            part = slice(t * TILE, (t + 1) * TILE)
            pe[part, :] = dot(one_hot(tiles[0][t], slots), emb_own, NN).astype(BF16)
            ps[part, :] = dot(one_hot(tiles[1][t], slots), emb_sib, NN).astype(BF16)
            ints = None
            for at in range(2):
                hot = one_hot(tiles[2 + at][t], slots)
                got = dot(hot, fac_parts[at][0], NN) + dot(hot, fac_parts[at][1], NN)
                ints = got if ints is None else ints + got
            pf[part, :] = ints * (FAC_MAX / LEVELS)

    def norms(one, two):
        one, two = one.astype(F32), two.astype(F32)
        return jnp.sum(one * one + two * two, axis=1, keepdims=True) * -0.5

    def fac_dot(left, right):
        return dot(jnp.concatenate([left[0], left[0], left[1]], axis=1), right, NT)

    high, low = split2(pf[...])
    right = jnp.concatenate([high, low, high], axis=1)
    pivot_lanes = norm_lanes(norms(pe[...], ps[...]), False)
    for start in range(0, width, TILE):
        part = slice(start, start + TILE)
        expo = dot(pe[part, :], pe[start:, :], NT) + dot(ps[part, :], ps[start:, :], NT)
        expo += dot(norm_lanes(norms(pe[part, :], ps[part, :]), True), pivot_lanes[start:, :], NT)
        row = lax.broadcasted_iota(jnp.int32, (TILE, width - start), 0)
        col = lax.broadcasted_iota(jnp.int32, (TILE, width - start), 1)
        value = jnp.exp(expo * scale) + jnp.where(row == col, ridge_weight, 0.0)
        t_ref[part, start:] = value - fac_dot(split2(pf[part, :]), right[start:, :])
    load_emb.wait()
    load_fac.wait()
    for start in range(0, own, TILE):
        part = slice(start, start + TILE)
        expo = dot(emb[part, :], pe[...], NT) + dot(es[part, :], ps[...], NT)
        expo += dot(norm_lanes(norms(emb[part, :], es[part, :]), True), pivot_lanes, NT)
        row = base + start + lax.broadcasted_iota(jnp.int32, (TILE, width), 0)
        value = jnp.exp(expo * scale) + jnp.where(row == pivots, ridge_weight, 0.0)
        q_ref[part, :] = value - fac_dot(split2(fo[part, :]), right)
    count = width // TILE
    tall = lax.broadcasted_iota(jnp.int32, (TILE, TILE), 0)
    flat = lax.broadcasted_iota(jnp.int32, (TILE, TILE), 1)

    def stack_left(pair, axis):
        return jnp.concatenate([pair[0], pair[0], pair[1]], axis=axis)

    def stack_right(pair, axis):
        return jnp.concatenate([pair[0], pair[1], pair[0]], axis=axis)

    def own_step(block, inverse, upper):
        here = slice(block * TILE, (block + 1) * TILE)
        fresh = dot(stack_left(split2(q_ref[:, here]), 1), stack_right(inverse, 1), NT)
        half, at = divmod(block * TILE, width // 2)
        out_ref[half, :, at : at + TILE] = fresh
        sq_ref[...] = fresh * fresh if block == 0 else sq_ref[...] + fresh * fresh
        if upper is not None:
            q_ref[:, (block + 1) * TILE :] -= dot(stack_left(split2(fresh), 1), stack_right(upper, 0), NN)

    late = None
    stores = [pltpu.make_async_copy(out_ref.at[i], out_any.at[i], so.at[i]) for i in range(2)]
    for block in range(count):
        here = slice(block * TILE, (block + 1) * TILE)
        s_ref[...] = t_ref[here, here]
        factor_tile(s_ref, cb_ref, pb_ref)
        if late is not None:
            own_step(*late)
        inverse = split2(jnp.where(flat <= tall, s_ref[...], 0.0))
        upper = None
        if block + 1 < count:
            rest = slice((block + 1) * TILE, width)
            upper = split2(dot(stack_left(inverse, 1), stack_right(split2(t_ref[here, rest]), 0), NN))
            for i in range(block + 1, count):
                rows = slice(i * TILE, (i + 1) * TILE)
                off = (i - block - 1) * TILE
                left = tuple(u[:, off : off + TILE] for u in upper)
                right = tuple(u[:, off:] for u in upper)
                t_ref[rows, i * TILE :] -= dot(stack_left(left, 0), stack_right(right, 0), TN)
        late = (block, inverse, upper)
        if block == count // 2:
            stores[0].start()
    own_step(*late)
    stores[1].start()
    hi, low = split2(sq_ref[...])
    ones = jnp.ones((SUB, TILE), BF16)
    removed = dot(ones, hi, NT) + dot(ones, low, NT)
    load_res.wait()
    ro_ref[...] = res_ref[...] - removed[0:1, :].reshape(own)
    stores.append(pltpu.make_async_copy(ro_ref, ro_any, so.at[2]))
    stores[2].start()
    for one in stores:
        one.wait()


def extend_call(pivots, a, b, emb, es, fo, residual, sides=(X_SIDE, SIDE)):
    width = pivots.size
    own, rank = fo.shape
    cols = emb.shape[1]
    vmem = pl.BlockSpec(memory_space=pltpu.VMEM)
    far = pl.BlockSpec(memory_space=pltpu.HBM)
    dma = pltpu.SemaphoreType.DMA
    return pl.pallas_call(
        functools.partial(extend, sides),
        out_shape=(
            jax.ShapeDtypeStruct((2, own, width // 2), F32),
            jax.ShapeDtypeStruct((own,), F32),
        ),
        in_specs=[far, vmem, vmem, far, vmem, far, far],
        out_specs=(far, far),
        scratch_shapes=[
            pltpu.VMEM(pivots.shape, jnp.int32),
            pltpu.VMEM((own,), F32),
            pltpu.VMEM((own,), F32),
            pltpu.VMEM((own, cols), BF16),
            pltpu.VMEM((own, rank), F32),
            pltpu.VMEM((2, own, width // 2), F32),
            pltpu.VMEM((width, cols), BF16),
            pltpu.VMEM((width, cols), BF16),
            pltpu.VMEM((width, rank), F32),
            pltpu.VMEM((width, width), F32),
            pltpu.VMEM((own, width), F32),
            pltpu.VMEM((TILE, TILE), F32),
            pltpu.VMEM((SUB * SUB, TILE), F32),
            pltpu.VMEM((SUB * SUB, TILE), F32),
            pltpu.VMEM((own, TILE), F32),
            dma,
            dma,
            dma,
            dma,
            dma((3,)),
        ],
        compiler_params=pltpu.CompilerParams(vmem_limit_bytes=ROOM),
        name="extend",
    )(pivots, a, b, emb, es, fo, residual)


def shards(sides, *given):
    embeddings, factor, residual_diag, pivots = (pltpu.with_memory_space_constraint(one, pltpu.HBM) for one in given)
    a, b, es = gather_call(embeddings, factor, pivots, sides)
    return extend_call(pivots, a, b, embeddings, es, factor, residual_diag, sides)


def solution(mesh):
    return jax.shard_map(
        functools.partial(shards, (X_SIDE, SIDE)),
        mesh=mesh,
        in_specs=(P("rows", "feat"), P(("rows", "feat"), None), P(("rows", "feat")), P()),
        out_specs=(P(None, ("rows", "feat"), None), P(("rows", "feat"))),
        check_vma=False,
    )
```
